32 devices in a mesh: dp: 4 (over y, x), fsdp: 8 (over z, core).
Axes of the slice: x: 2, y: 2, z: 4, core: 2. Of those that a mesh axis runs over, the one named last changes fastest.
Arguments:
- queries: bfloat16 [8192, 1024], P(('dp', 'fsdp')), may hold values from -96 to 96
- keys: bfloat16 [8192, 1024], P(('dp', 'fsdp')), may hold values from -6 to 6
- values: bfloat16 [8192, 1024], P(('dp', 'fsdp')), may hold values from -6 to 6
- cotangent: bfloat16 [8192, 3072], P(('dp', 'fsdp')), may hold values from -6 to 6
- w_out: bfloat16 [1024, 3072], P('fsdp'), may hold values from -0.1875 to 0.1875
- counts: int32 [32, 4], P(('dp', 'fsdp')), may hold values from 1 to 128, 256 in all within a row
- dests: int32 [32, 4], P(('dp', 'fsdp')), may hold values from 0 to 3, each once within a row
Outputs:
- grad_queries: bfloat16 [8192, 1024], P(('dp', 'fsdp'))
- grad_keys: bfloat16 [8192, 1024], P(('dp', 'fsdp'))
- grad_values: bfloat16 [8192, 1024], P(('dp', 'fsdp'))
- attended: bfloat16 [4, 8, 4, 128, 1024], P('dp', 'fsdp')
- weight_grad: float32 [1024, 3072], P('fsdp')
The draws below stay inside these ranges and needn't reach their ends.
Inputs may be any that keep to these rules, and one draw needn't show every extreme that they name: `counts`: each device's 4 images fill its 256 rows; on every device one image has exactly 128 rows. `dests`: each device assigns exactly one image to every data group.
All inputs are finite; a program needn't handle non-finite values.
Results may differ from the reference program's by a relative error of at most 0.015.
Values may be sent and summed in bfloat16 or wider, within the bound.
No kernel may reach another device: no remote copies, remote signals or barrier semaphores. Data moves between devices by JAX's collectives and lax.ppermute only.
A program may use at most 128 MiB of HBM per device.

```python
import math
import jax
import jax.numpy as jnp
import numpy as np
from jax import lax

D = 3072
HEADS = 8
HD = 1024
LMAX = 128
GROUPS = 4
ROWS_DEV = 256
TOKENS = 8192
N_DP = 4
N_FSDP = 8
DEVICES = 32


def shared_keys(key):
    return jax.random.normal(key, (TOKENS, HD), jnp.float32)


def draw_keys(key, part):
    base = shared_keys(key)
    return jnp.clip(base, -6.0, 6.0).astype(jnp.bfloat16)


def draw_queries(key, part):
    key = jax.random.fold_in(key, 23)
    first = jax.random.fold_in(key, 0)
    return jnp.clip(jax.random.normal(first, (TOKENS, HD), jnp.float32), -6.0, 6.0).astype(jnp.bfloat16)


def block_levels(key, extent, pieces, least, largest):
    level = 1.0
    for position, shards_of in pieces:
        heights = jax.random.uniform(jax.random.fold_in(jax.random.fold_in(key, 6), position), (shards_of,), jnp.float32, least / len(pieces), largest / len(pieces))
        level = level * jnp.repeat(jnp.exp(heights), extent[position] // shards_of).reshape((-1,) + (1,) * (len(extent) - 1 - position))
    return level


def profile(amount, total, most, skew):
    weights = [(1 << 20) // math.isqrt(standing ** skew) + 1 for standing in range(2, amount + 1)]
    spare, holding = total - most - (amount - 1), [1] * (amount - 1)
    while spare > 0:
        movable = [i for i in range(amount - 1) if holding[i] < most]
        mass, remaining = sum([weights[i] for i in movable]), spare
        for i in movable:
            extra = min(most - holding[i], max(1, remaining * weights[i] // mass), spare)
            holding[i] = holding[i] + extra
            spare = spare - extra
    return np.array([most] + holding)


def uneven(key, amount, total, reach, slope):
    if amount == 2:
        one = jax.random.randint(key, (), max(1, total - reach), min(reach, total - 1) + 1)
        return jnp.stack([one, total - one])
    sizes = jnp.asarray(profile(amount, total, reach, slope), jnp.int32)
    twos = (amount - 1) // 2
    giver, receiver = sizes[1:1 + 2 * twos:2], sizes[2:2 + 2 * twos:2]
    margin = jnp.minimum(giver - 1, reach - receiver)
    moved = jax.random.randint(jax.random.fold_in(key, 1), (twos,), 0, 1 << 20) % (margin + 1)
    sizes = sizes.at[1:1 + 2 * twos:2].set(giver - moved).at[2:2 + 2 * twos:2].set(receiver + moved)
    return sizes[jax.random.permutation(jax.random.fold_in(key, 2), amount)]


def bell_draw(own_key, dims, scale, reach, cuts=(), kind=jnp.bfloat16):
    entries = jax.random.normal(own_key, dims, jnp.float32) * scale
    if len(cuts) > 0:
        entries = block_levels(own_key, dims, cuts, -0.22, 0.18) * entries
    return jnp.clip(entries, min=-reach, max=reach).astype(kind)


def setup_inputs(seed: int = 0) -> dict:
    key_of = jax.random.split(jax.random.key(seed), 8)
    queries = draw_queries(jax.random.fold_in(key_of[7], 71), 0)
    keys = draw_keys(jax.random.fold_in(key_of[7], 71), 0)
    values = bell_draw(key_of[2], (TOKENS, HD), 1.0, 6.0, ((0, 32),))
    cotangent = bell_draw(key_of[3], (TOKENS, D), 1.0, 6.0, ((0, 32),))
    w_out = bell_draw(key_of[4], (HD, D), HD ** -0.5, 0.1875, ((0, 8),))
    counts = jax.vmap(lambda own: uneven(own, GROUPS, ROWS_DEV, LMAX, 2))(jax.random.split(key_of[5], DEVICES)).reshape((DEVICES, GROUPS)).astype(jnp.int32)
    dests = jax.vmap(lambda own: jax.random.permutation(own, GROUPS))(jax.random.split(key_of[6], DEVICES)).reshape((DEVICES, GROUPS)).astype(jnp.int32)
    return {"queries": queries, "keys": keys, "values": values, "cotangent": cotangent, "w_out": w_out, "counts": counts, "dests": dests}


def pick(table, index):
    places = jnp.arange(table.shape[0], dtype=jnp.int32)
    chosen = jnp.where(index[:, None] == places[None, :], table[None, :], 0)
    return jnp.sum(chosen, axis=1).astype(jnp.int32)


def fill_slots(image_rows, sizes, starts, chosen, length):
    places = jnp.arange(length, dtype=jnp.int32)
    first = pick(starts, chosen)
    size = pick(sizes, chosen)
    row_index = jnp.minimum(first[:, None] + places[None, :], image_rows.shape[0] - 1).astype(jnp.int32)
    taken = jnp.take(image_rows, row_index.reshape(-1), axis=0)
    taken = taken.reshape(chosen.shape[0], length, image_rows.shape[1])
    live = places[None, :] < size[:, None]
    return jnp.where(live[:, :, None], taken, jnp.zeros_like(taken)), size


def read_slots(slot_data, sizes, starts, slot_of_image, rows):
    slots, length, width = slot_data.shape
    places = jnp.arange(rows, dtype=jnp.int32)
    ends = starts + sizes
    image = jnp.sum((ends[None, :] <= places[:, None]).astype(jnp.int32), axis=1).astype(jnp.int32)
    first = pick(starts, image)
    slot = pick(slot_of_image, image)
    flat = (slot * length + places - first).astype(jnp.int32)
    return jnp.take(slot_data.reshape(slots * length, width), flat, axis=0)


def attend_images(query_slots, key_slots, value_slots, grad_slots, lengths):
    slots, length, width = query_slots.shape
    head_size = width // HEADS
    scale = head_size ** -0.5
    shape = (slots, length, HEADS, head_size)
    query_h = query_slots.reshape(shape).astype(jnp.float32)
    key_h = key_slots.reshape(shape).astype(jnp.float32)
    value_h = value_slots.reshape(shape).astype(jnp.float32)
    grad_h = grad_slots.reshape(shape).astype(jnp.float32)
    scores = jnp.einsum("gqhe,gkhe->ghqk", query_h, key_h) * scale
    places = jnp.arange(length, dtype=jnp.int32)
    live = places[None, :] < lengths[:, None]
    scores = jnp.where(live[:, None, None, :], scores, -1e30)
    top = jnp.max(scores, axis=-1, keepdims=True)
    weights = jnp.exp(scores - top)
    probs = weights / jnp.sum(weights, axis=-1, keepdims=True)
    probs_b = lax.optimization_barrier(probs.astype(jnp.bfloat16)).astype(jnp.float32)
    outputs = jnp.einsum("ghqk,gkhe->gqhe", probs_b, value_h)
    outputs = jnp.where(live[:, :, None, None], outputs, 0.0)
    dprobs = jnp.einsum("gqhe,gkhe->ghqk", grad_h, value_h)
    delta = jnp.sum(probs * dprobs, axis=-1, keepdims=True)
    dscores = lax.optimization_barrier((probs * (dprobs - delta) * scale).astype(jnp.bfloat16)).astype(jnp.float32)
    grad_q = jnp.einsum("ghqk,gkhe->gqhe", dscores, key_h)
    grad_k = jnp.einsum("ghqk,gqhe->gkhe", dscores, query_h)
    grad_v = jnp.einsum("ghqk,gqhe->gkhe", probs_b, grad_h)
    flat = (slots, length, width)
    return (grad_q.reshape(flat).astype(jnp.bfloat16), grad_k.reshape(flat).astype(jnp.bfloat16),
            grad_v.reshape(flat).astype(jnp.bfloat16), outputs.reshape(flat).astype(jnp.bfloat16))


def reference(queries, keys, values, cotangent, w_out, counts, dests):
    grad_rows = jnp.dot(cotangent, w_out.T, preferred_element_type=jnp.float32).astype(jnp.bfloat16)
    shape = (DEVICES, ROWS_DEV, HD)

    def one_device(pack):
        query_rows, key_rows, value_rows, grad_in, sizes, targets = pack
        sizes = sizes.astype(jnp.int32)
        starts = (jnp.cumsum(sizes) - sizes).astype(jnp.int32)
        order = jnp.arange(GROUPS, dtype=jnp.int32)
        query_slots, size = fill_slots(query_rows, sizes, starts, order, LMAX)
        key_slots, size = fill_slots(key_rows, sizes, starts, order, LMAX)
        value_slots, size = fill_slots(value_rows, sizes, starts, order, LMAX)
        grad_slots, size = fill_slots(grad_in, sizes, starts, order, LMAX)
        grad_q, grad_k, grad_v, outputs = attend_images(query_slots, key_slots, value_slots, grad_slots, size)
        rows_q = read_slots(grad_q, sizes, starts, order, ROWS_DEV)
        rows_k = read_slots(grad_k, sizes, starts, order, ROWS_DEV)
        rows_v = read_slots(grad_v, sizes, starts, order, ROWS_DEV)
        rows_o = read_slots(outputs, sizes, starts, order, ROWS_DEV)
        chosen = jnp.sum(jnp.where(targets[None, :] == order[:, None], order[None, :], 0), axis=1).astype(jnp.int32)
        sent = jnp.take(outputs, chosen, axis=0)
        return rows_q, rows_k, rows_v, rows_o, sent

    packs = (queries.reshape(shape), keys.reshape(shape), values.reshape(shape),
             grad_rows.reshape(shape), counts, dests)
    rows_q, rows_k, rows_v, rows_o, sent = lax.map(one_device, packs)
    grad_scale = TOKENS ** -0.5

    def add_term(total, pack):
        out_rows, grad_in = pack
        term = jnp.dot(out_rows.T, grad_in, preferred_element_type=jnp.float32) * grad_scale
        term = lax.optimization_barrier(term.astype(jnp.bfloat16))
        return total + term.astype(jnp.float32), None

    start = jnp.zeros((HD, D), jnp.float32)
    weight_grad, unused = lax.scan(add_term, start, (rows_o, cotangent.reshape(DEVICES, ROWS_DEV, D)))
    attended = sent.reshape(N_DP, N_FSDP, GROUPS, LMAX, HD).transpose(2, 1, 0, 3, 4)
    return (rows_q.reshape(TOKENS, HD), rows_k.reshape(TOKENS, HD), rows_v.reshape(TOKENS, HD),
            attended, weight_grad)
```

```python
import functools

import jax
import jax.numpy as jnp
from jax import lax
from jax.experimental import pallas as pl
from jax.experimental.pallas import tpu as pltpu
from jax.sharding import PartitionSpec as P

HEADS = 8
LMAX = 128
HEAD = 128
HEADER = 16
VMEM_LIMIT = 56 * 1024 * 1024

F32 = jnp.float32
BF16 = jnp.bfloat16
SMEM = pl.BlockSpec(memory_space=pltpu.SMEM)
VMEM = pl.BlockSpec(memory_space=pltpu.VMEM)


def dot(a, b, ca, cb):
    return lax.dot_general(a, b, (((ca,), (cb,)), ((), ())), preferred_element_type=F32)


def call(kernel, out_shape, in_specs, flops, moved, transcendentals=0, name=None):
    single = not isinstance(out_shape, (list, tuple))
    return pl.pallas_call(
        kernel,
        out_shape=out_shape,
        in_specs=in_specs,
        out_specs=VMEM if single else [VMEM] * len(out_shape),
        compiler_params=pltpu.CompilerParams(vmem_limit_bytes=VMEM_LIMIT),
        cost_estimate=pl.CostEstimate(
            flops=flops, bytes_accessed=moved, transcendentals=transcendentals
        ),
        name=name,
    )


def shaped(*shape, dtype=BF16):
    return jax.ShapeDtypeStruct(shape, dtype)


def image_of(index, counts_ref):
    image = jnp.zeros_like(index)
    end = 0
    for g in range(counts_ref.shape[1]):
        end = end + counts_ref[0, g]
        image = image + (index >= end).astype(jnp.int32)
    return image


def forward_kernel(counts_ref, dests_ref, q_ref, k_ref, v_ref, out_ref, probs_ref):
    rows = q_ref.shape[0]
    scale = float(HEAD) ** -0.5
    image_r = image_of(lax.broadcasted_iota(jnp.int32, (rows, 1), 0), counts_ref)
    image_c = image_of(lax.broadcasted_iota(jnp.int32, (1, rows), 1), counts_ref)
    same = image_r == image_c
    for h in range(HEADS):
        cols = pl.ds(h * HEAD, HEAD)
        scores = dot(q_ref[:, cols], k_ref[:, cols], 1, 1) * scale
        scores = jnp.where(same, scores, -1e30)
        top = jnp.max(scores, axis=1, keepdims=True)
        weights = jnp.exp(scores - top)
        probs = weights * (1.0 / jnp.sum(weights, axis=1, keepdims=True))
        probs_ref[h] = probs
        out_ref[:rows, cols] = dot(probs.astype(BF16), v_ref[:, cols], 1, 0).astype(BF16)
    width = q_ref.shape[1]
    index = lax.broadcasted_iota(jnp.int32, (HEADER, width), 1)
    place, group = index, jnp.full((HEADER, width), dests_ref[0, 0], jnp.int32)
    end = 0
    for g in range(counts_ref.shape[1] - 1):
        end = end + counts_ref[0, g]
        past = index >= end
        place = jnp.where(past, place - counts_ref[0, g], place)
        group = jnp.where(past, dests_ref[0, g + 1], group)
    line = lax.broadcasted_iota(jnp.int32, (HEADER, width), 0)
    header = jnp.where(index < rows, jnp.where(line == 0, place, jnp.where(line == 1, group, 0)), -1)
    out_ref[rows:, :] = header.astype(F32).astype(BF16)


def forward(counts, dests, queries, keys, values):
    rows, width = queries.shape
    return call(
        forward_kernel,
        [shaped(rows + HEADER, width), shaped(HEADS, rows, rows, dtype=F32)],
        [SMEM, SMEM, VMEM, VMEM, VMEM],
        4 * rows * rows * width,
        8 * rows * width + 4 * HEADS * rows * rows,
        HEADS * rows * rows,
        name="forward",
    )(counts, dests, queries, keys, values)


def backward_kernel(split, *refs):
    if split:
        at_ref, *refs = refs
    probs_ref, q_ref, k_ref, v_ref, *grads, dq_ref, dk_ref, dv_ref = refs
    scale = float(HEAD) ** -0.5
    for h in range(HEADS):
        cols = pl.ds(h * HEAD, HEAD)
        if split:
            part = pl.ds(h // 2 * HEAD, HEAD)
            grad = jnp.where(at_ref[3] == h % 2, grads[0][:, part], grads[1][:, part])
        else:
            grad = grads[0][:, cols]
        probs = probs_ref[h]
        dprobs = dot(grad, v_ref[:, cols], 1, 1)
        delta = jnp.sum(probs * dprobs, axis=1, keepdims=True)
        dscores = (probs * (dprobs - delta) * scale).astype(BF16)
        dq_ref[:, cols] = dot(dscores, k_ref[:, cols], 1, 0).astype(BF16)
        dk_ref[:, cols] = dot(dscores, q_ref[:, cols], 0, 0).astype(BF16)
        dv_ref[:, cols] = dot(probs.astype(BF16), grad, 0, 0).astype(BF16)


def backward(at, probs, queries, keys, values, *grads):
    rows, width = queries.shape
    split = len(grads) == 2
    return call(
        functools.partial(backward_kernel, split),
        [shaped(rows, width)] * 3,
        ([SMEM] if split else []) + [VMEM] * (4 + len(grads)),
        8 * rows * rows * width,
        14 * rows * width + 4 * HEADS * rows * rows,
        name="backward",
    )(*(([at] if split else [])), probs, queries, keys, values, *grads)


def attended_kernel(at_ref, *refs):
    *sources, out_ref = refs
    rows = sources[0].shape[0] - HEADER
    me = at_ref[0]
    place = lax.broadcasted_iota(jnp.int32, (LMAX, rows), 0)
    for s, source in enumerate(sources):
        header = source[rows:, :rows].astype(F32).astype(jnp.int32)
        chosen = (header[0:1] == place) & (header[1:2] == me)
        chosen = jnp.where(chosen, 1.0, 0.0).astype(BF16)
        out_ref[me ^ s] = dot(chosen, source[:rows, :], 1, 0).astype(BF16)


def attended_of(at, sources):
    width = sources[0].shape[1]
    rows = sources[0].shape[0] - HEADER
    return call(
        attended_kernel,
        shaped(len(sources), LMAX, width),
        [SMEM] + [VMEM] * len(sources),
        2 * len(sources) * LMAX * rows * width,
        2 * len(sources) * (rows + LMAX) * width,
        name="attended",
    )(at, *sources)


def slots_kernel(counts_ref, dests_ref, out_ref, slots_ref):
    rows = out_ref.shape[0] - HEADER
    groups = counts_ref.shape[1]
    place = lax.broadcasted_iota(jnp.int32, (LMAX, rows), 0)
    index = lax.broadcasted_iota(jnp.int32, (LMAX, rows), 1)
    start = 0
    for g in range(groups):
        count = counts_ref[0, g]
        chosen = (index == place + start) & (place < count)
        chosen = jnp.where(chosen, 1.0, 0.0).astype(BF16)
        slots_ref[dests_ref[0, g]] = dot(chosen, out_ref[:rows, :], 1, 0).astype(BF16)
        start = start + count


def term_kernel(scale, at_ref, cot_ref, *refs):
    *sources, c1_ref, c2_ref, c3_ref, keep_ref, send_ref = refs
    rows = cot_ref.shape[0]
    part = c1_ref.shape[1]
    me, z, c = at_ref[0], at_ref[2], at_ref[3]
    own = cot_ref[:, pl.ds(pl.multiple_of(me * part, part), part)]
    for m in range(4):
        pair = pl.ds(pl.multiple_of((z ^ m) * 2 * HEAD, 2 * HEAD), 2 * HEAD)
        total = dot(sources[0][:rows, pair], own, 0, 0)
        for source, cot in zip(sources[1:], (c1_ref, c2_ref, c3_ref)):
            total = total + dot(source[:rows, pair], cot[...], 0, 0)
        total = total * scale
        low, high = total[:HEAD], total[HEAD:]
        keep_ref[m] = jnp.where(c == 0, low, high)
        send_ref[m] = jnp.where(c == 0, high, low).astype(BF16)


def rows_kernel(at_ref, cot_ref, other_ref, own_ref, z1_ref, z2_ref, z3_ref, x_ref, y_ref, keep_ref, send_ref):
    me, z = at_ref[0], at_ref[2]
    part = x_ref.shape[1]
    x, y = me & 1, me >> 1

    def quarter(ref, q):
        return ref[:, pl.ds(pl.multiple_of(q * part, part), part)]

    for tokens, out in ((other_ref, send_ref), (cot_ref, keep_ref)):
        for m, near in enumerate((own_ref, z1_ref, z2_ref, z3_ref)):
            if m == 0:
                total = dot(tokens[...], near[...], 1, 1)
            else:
                block = pl.ds((m - 1) * HEAD, HEAD)
                total = dot(quarter(tokens, x), near[:, :part], 1, 1)
                total = total + dot(quarter(tokens, 2 + y), near[:, part:], 1, 1)
                total = total + dot(quarter(tokens, 1 - x), x_ref[block], 1, 1)
                total = total + dot(quarter(tokens, 3 - y), y_ref[block], 1, 1)
            out[:, pl.ds(pl.multiple_of((z ^ m) * HEAD, HEAD), HEAD)] = total.astype(BF16)


def place_kernel(at_ref, *refs):
    *pieces, out_ref = refs
    part = pieces[0].shape[1]
    for s, piece in enumerate(pieces):
        columns = pl.ds(pl.multiple_of((at_ref[0] ^ s) * part, part), part)
        out_ref[:, columns] = piece[...].astype(F32)


def swap(value, axis, mask):
    size = lax.axis_size(axis)
    return lax.ppermute(value, axis, [(i, i ^ mask) for i in range(size)])


def plane_body(queries, keys, values, cotangent, w_out, counts, dests):
    rows, width = queries.shape
    depth = cotangent.shape[1]
    part = depth // 4
    me, f = lax.axis_index("dp"), lax.axis_index("fsdp")
    z, c = f // 2, f % 2
    at = jnp.stack([me, f, z, c]).astype(jnp.int32)
    tokens = rows * lax.axis_size("dp") * lax.axis_size("fsdp")

    cots = [
        swap(lax.dynamic_slice_in_dim(cotangent, (me ^ s) * part, part, axis=1), "dp", s)
        for s in (1, 2, 3)
    ]
    cot_other = swap(cotangent, "fsdp", 1)
    x, y = me % 2, me // 2
    mine = jnp.concatenate(
        [
            lax.dynamic_slice_in_dim(w_out, x * part, part, axis=1),
            lax.dynamic_slice_in_dim(w_out, (2 + y) * part, part, axis=1),
        ],
        axis=1,
    )
    near = [swap(mine, "fsdp", 2 * m) for m in (1, 2, 3)]

    out, probs = forward(counts, dests, queries, keys, values)
    outs = [out] + [swap(out, "dp", s) for s in (1, 2, 3)]

    keep, send = call(
        functools.partial(term_kernel, float(tokens) ** -0.5),
        [shaped(4, HEAD, part, dtype=F32), shaped(4, HEAD, part)],
        [SMEM] + [VMEM] * 8,
        2 * 4 * rows * width * part,
        8 * rows * (width + part) + 6 * width * part // 2,
        name="term",
    )(at, cotangent, *outs, *cots)
    sums = keep + swap(send, "fsdp", 1).astype(F32)
    apart = [swap(sums[m].astype(BF16), "fsdp", 2 * m) for m in (1, 2, 3)]

    attended = attended_of(at, outs)

    from_x = swap(jnp.concatenate([w[:, :part] for w in near], axis=0), "dp", 1)
    from_y = swap(jnp.concatenate([w[:, part:] for w in near], axis=0), "dp", 2)
    grad_keep, grad_send = call(
        rows_kernel,
        [shaped(rows, width // 2)] * 2,
        [SMEM] + [VMEM] * 8,
        2 * rows * width * depth,
        2 * (2 * rows * depth + width * depth // 2 + rows * width),
        name="grad_rows",
    )(at, cotangent, cot_other, w_out, *near, from_x, from_y)
    grad_other = swap(grad_send, "fsdp", 1)
    grads = backward(at, probs, queries, keys, values, grad_keep, grad_other)

    shard = sums[0]
    for piece in apart:
        shard = shard + piece.astype(F32)
    shard = shard.astype(BF16)
    pieces = [shard] + [swap(shard, "dp", s) for s in (1, 2, 3)]
    weight_grad = call(
        place_kernel,
        shaped(HEAD, depth, dtype=F32),
        [SMEM] + [VMEM] * 4,
        HEAD * depth,
        6 * HEAD * depth,
        name="place",
    )(at, *pieces)
    return (*grads, attended[None, None], weight_grad)


def body(queries, keys, values, cotangent, w_out, counts, dests):
    rows, width = queries.shape
    tokens = rows * lax.axis_size("dp") * lax.axis_size("fsdp")
    out, probs = forward(counts, dests, queries, keys, values)
    slots = call(
        slots_kernel,
        shaped(counts.shape[1], LMAX, width),
        [SMEM, SMEM, VMEM],
        2 * counts.shape[1] * LMAX * rows * width,
        4 * rows * width,
        name="slots",
    )(counts, dests, out)
    attended = lax.all_to_all(slots, "dp", split_axis=0, concat_axis=0, tiled=True)
    product = dot(out[:rows], cotangent, 0, 0) * float(tokens) ** -0.5
    shard = lax.psum_scatter(product.astype(BF16), "fsdp", scatter_dimension=0, tiled=True)
    weight_grad = lax.psum(shard, "dp").astype(F32)
    grad_rows = dot(cotangent, lax.all_gather(w_out, "fsdp", axis=0, tiled=True), 1, 1).astype(BF16)
    grads = backward(None, probs, queries, keys, values, grad_rows)
    return (*grads, attended[None, None], weight_grad)


def solution(mesh):
    placed = (
        P(("dp", "fsdp"), None),
        P(("dp", "fsdp"), None),
        P(("dp", "fsdp"), None),
        P(("dp", "fsdp"), None),
        P("fsdp", None),
        P(("dp", "fsdp"), None),
        P(("dp", "fsdp"), None),
    )
    plane = mesh.shape["dp"] == 4 and mesh.shape["fsdp"] == HEADS
    return jax.shard_map(
        plane_body if plane else body,
        mesh=mesh,
        in_specs=placed,
        out_specs=(
            P(("dp", "fsdp"), None),
            P(("dp", "fsdp"), None),
            P(("dp", "fsdp"), None),
            P("dp", "fsdp", None, None, None),
            P("fsdp", None),
        ),
        check_vma=False,
    )
```

```python
import functools

import jax
import jax.numpy as jnp
from jax import lax
from jax.experimental import pallas as pl
from jax.experimental.pallas import tpu as pltpu
from jax.sharding import PartitionSpec as P

HEADS = 8
LMAX = 128
HEAD = 128
HEADER = 16
MIB = 1024 * 1024

F32 = jnp.float32
BF16 = jnp.bfloat16
SMEM = pl.BlockSpec(memory_space=pltpu.SMEM)
VMEM = pl.BlockSpec(memory_space=pltpu.VMEM)
ANY = pl.BlockSpec(memory_space=pl.ANY)
HBM = pl.BlockSpec(memory_space=pltpu.HBM)


def dot(a, b, ca, cb):
    return lax.dot_general(a, b, (((ca,), (cb,)), ((), ())), preferred_element_type=F32)


def call(kernel, out_shape, args, flops, moved, exps=0, name=None, mib=24, after=(), **more):
    single = not isinstance(out_shape, (list, tuple))
    given = len(args)
    more.setdefault("in_specs", [SMEM if a.dtype == jnp.int32 else VMEM for a in args])
    more.setdefault("out_specs", VMEM if single else [VMEM] * len(out_shape))
    more["in_specs"] = more["in_specs"] + [ANY] * len(after)

    def run(*refs):
        kernel(*refs[:given], *refs[given + len(after) :])

    return pl.pallas_call(
        run,
        out_shape=out_shape,
        compiler_params=pltpu.CompilerParams(vmem_limit_bytes=mib * MIB),
        cost_estimate=pl.CostEstimate(flops=flops, bytes_accessed=moved, transcendentals=exps),
        name=name,
        **more,
    )(*args, *after)


def shaped(*shape, dtype=BF16):
    return jax.ShapeDtypeStruct(shape, dtype)


def image_of(index, counts_ref):
    image = jnp.zeros_like(index)
    end = 0
    for g in range(counts_ref.shape[1]):
        end = end + counts_ref[0, g]
        image = image + (index >= end).astype(jnp.int32)
    return image


def image_rows(start, count, out):
    rows = out.shape[0]
    place = lax.broadcasted_iota(jnp.int32, (LMAX, rows), 0)
    index = lax.broadcasted_iota(jnp.int32, (LMAX, rows), 1)
    chosen = (index == place + start) & (place < count)
    return dot(jnp.where(chosen, 1.0, 0.0).astype(BF16), out, 1, 0).astype(BF16)


def probs_kernel(counts_ref, q_ref, k_ref, probs_ref):
    rows = q_ref.shape[0]
    scale = float(HEAD) ** -0.5
    image_r = image_of(lax.broadcasted_iota(jnp.int32, (rows, 1), 0), counts_ref)
    image_c = image_of(lax.broadcasted_iota(jnp.int32, (1, rows), 1), counts_ref)
    same = image_r == image_c
    for h in range(HEADS):
        cols = pl.ds(h * HEAD, HEAD)
        scores = dot(q_ref[:, cols], k_ref[:, cols], 1, 1) * scale
        scores = jnp.where(same, scores, -1e30)
        top = jnp.max(scores, axis=1, keepdims=True)
        weights = jnp.exp(scores - top)
        probs_ref[h] = weights * (1.0 / jnp.sum(weights, axis=1, keepdims=True))


def outputs_of(probs_ref, v_ref, out_ref):
    rows = v_ref.shape[0]
    for h in range(HEADS):
        cols = pl.ds(h * HEAD, HEAD)
        out_ref[:rows, cols] = dot(probs_ref[h].astype(BF16), v_ref[:, cols], 1, 0).astype(BF16)


def outputs_kernel(at_ref, counts_ref, dests_ref, probs_ref, v_ref, out_ref, far_ref):
    outputs_of(probs_ref, v_ref, out_ref)
    rows, width = v_ref.shape
    index = lax.broadcasted_iota(jnp.int32, (HEADER, width), 1)
    line = lax.broadcasted_iota(jnp.int32, (HEADER, width), 0)
    place, group = index, jnp.full((HEADER, width), dests_ref[0, 0], jnp.int32)
    start, far_start, far_count = 0, 0, 0
    for g in range(counts_ref.shape[1]):
        count, dest = counts_ref[0, g], dests_ref[0, g]
        far = dest == (at_ref[0] ^ 3)
        far_start = jnp.where(far, start, far_start)
        far_count = jnp.where(far, count, far_count)
        past = index >= start
        group = jnp.where(past, dest, group)
        place = jnp.where(past, index - start, place)
        start = start + count
    header = jnp.where(line == 0, place, jnp.where(line == 1, group, 0))
    header = jnp.where(index < rows, header, -1)
    out_ref[rows:, :] = header.astype(F32).astype(BF16)
    far_ref[...] = image_rows(far_start, far_count, out_ref[:rows, :])


def slots_kernel(counts_ref, dests_ref, probs_ref, v_ref, out_ref, slots_ref):
    outputs_of(probs_ref, v_ref, out_ref)
    start = 0
    for g in range(counts_ref.shape[1]):
        count = counts_ref[0, g]
        slots_ref[dests_ref[0, g]] = image_rows(start, count, out_ref[...])
        start = start + count


def probs_of(counts, queries, keys, **more):
    rows, width = queries.shape
    return call(
        probs_kernel,
        shaped(HEADS, rows, rows, dtype=F32),
        [counts, queries, keys],
        2 * rows * rows * width,
        4 * rows * width + 4 * HEADS * rows * rows,
        HEADS * rows * rows,
        name="probs",
        **more,
    )


def backward_kernel(split, *refs):
    if split:
        at_ref, *refs = refs
    probs_ref, q_ref, k_ref, v_ref, *grads, dq_ref, dk_ref, dv_ref = refs
    scale = float(HEAD) ** -0.5
    for h in range(HEADS):
        cols = pl.ds(h * HEAD, HEAD)
        if split:
            part = pl.ds(h // 2 * HEAD, HEAD)
            grad = jnp.where(at_ref[3] == h % 2, grads[0][:, part], grads[1][:, part])
        else:
            grad = grads[0][:, cols]
        probs = probs_ref[h]
        dprobs = dot(grad, v_ref[:, cols], 1, 1)
        delta = jnp.sum(probs * dprobs, axis=1, keepdims=True)
        dscores = (probs * (dprobs - delta) * scale).astype(BF16)
        dq_ref[:, cols] = dot(dscores, k_ref[:, cols], 1, 0).astype(BF16)
        dk_ref[:, cols] = dot(dscores, q_ref[:, cols], 0, 0).astype(BF16)
        dv_ref[:, cols] = dot(probs.astype(BF16), grad, 0, 0).astype(BF16)


def backward(at, probs, queries, keys, values, *grads, mib=24):
    rows, width = queries.shape
    split = at is not None
    return call(
        functools.partial(backward_kernel, split),
        [shaped(rows, width)] * 3,
        ([at] if split else []) + [probs, queries, keys, values, *grads],
        8 * rows * rows * width,
        14 * rows * width + 4 * HEADS * rows * rows,
        name="backward",
        mib=mib,
    )


def attended_kernel(at_ref, own_ref, x_ref, y_ref, far_ref, out_ref):
    rows = own_ref.shape[0] - HEADER
    me = at_ref[0]
    place = lax.broadcasted_iota(jnp.int32, (LMAX, rows), 0)
    for s, source in enumerate((own_ref, x_ref, y_ref)):
        header = source[rows:, :rows].astype(F32).astype(jnp.int32)
        chosen = (header[0:1] == place) & (header[1:2] == me)
        chosen = jnp.where(chosen, 1.0, 0.0).astype(BF16)
        out_ref[me ^ s] = dot(chosen, source[:rows, :], 1, 0).astype(BF16)
    out_ref[me ^ 3] = far_ref[...]


def columns(ref, start, size):
    return ref[:, pl.ds(pl.multiple_of(start, HEAD), size)]


def copy_all(pairs, sems):
    copies = [pltpu.make_async_copy(a, b, sems.at[i]) for i, (a, b) in enumerate(pairs)]
    for copy in copies:
        copy.start()
    for copy in copies:
        copy.wait()


def quarters_kernel(cot_ref, x_ref, y_ref, sems):
    part = x_ref.shape[1]
    me = lax.axis_index("dp")
    x, y = me & 1, me >> 1
    starts = (1 - x) * part, (3 - y) * part
    pairs = [
        (cot_ref.at[:, pl.ds(pl.multiple_of(start, HEAD), part)], out)
        for start, out in zip(starts, (x_ref, y_ref))
    ]
    copy_all(pairs, sems)


def mine_kernel(w_ref, out_ref, sems):
    part = out_ref.shape[2] // 2
    me = lax.axis_index("dp")
    starts = (me & 1) * part, (2 + (me >> 1)) * part
    pairs = [
        (w_ref.at[:, pl.ds(pl.multiple_of(start, HEAD), part)], out_ref.at[i, :, pl.ds(j * part, part)])
        for i in range(out_ref.shape[0])
        for j, start in enumerate(starts)
    ]
    copy_all(pairs, sems)


def pack_kernel(at_ref, line_ref, x_ref, y_ref):
    part = x_ref.shape[1]
    for m in range(1, 4):
        block = pl.ds((m - 1) * HEAD, HEAD)
        x_ref[block] = line_ref[at_ref[2] ^ m, :, :part]
        y_ref[block] = line_ref[at_ref[2] ^ m, :, part:]


def term_kernel(
    scale, at_ref, cot_ref, own_ref, x_ref, y_ref, cx_ref, cy_ref, keep_ref, keep_a_ref, keep_b_ref, first_ref, second_ref
):
    rows, part = cx_ref.shape
    half = part // 2
    x, y, z, c = at_ref[0] & 1, at_ref[0] >> 1, at_ref[2], at_ref[3]
    for r, out in ((1, first_ref), (0, second_ref)):
        for b, (near, cot, inner, outer) in enumerate(
            ((x_ref, cx_ref, y ^ r, x * part), (y_ref, cy_ref, x ^ r, (2 + y) * part))
        ):
            own_cot = columns(cot_ref, outer + inner * half, half)
            near_cot = columns(cot, inner * half, half)
            for m in range(4):
                pair = (z ^ m) * 2 * HEAD
                total = dot(columns(own_ref, pair, 2 * HEAD)[:rows], own_cot, 0, 0)
                total = total + dot(columns(near, pair, 2 * HEAD)[:rows], near_cot, 0, 0)
                total = total * scale
                low, high = total[:HEAD], total[HEAD:]
                kept = jnp.where(c == 0, low, high)
                if r == 1:
                    keep_ref[b, m] = kept
                else:
                    (keep_a_ref, keep_b_ref)[b][m] = kept
                out[b, m] = jnp.where(c == 0, high, low).astype(BF16)


def rows_own_kernel(cot_ref, other_ref, own_ref, out_ref):
    rows = cot_ref.shape[0]
    out_ref[:rows] = dot(cot_ref[...], own_ref[...], 1, 1).astype(BF16)
    out_ref[rows:] = dot(other_ref[...], own_ref[...], 1, 1).astype(BF16)


def rows_early_kernel(at_ref, cot_ref, other_ref, line_ref, out_ref):
    me, z, rows = at_ref[0], at_ref[2], cot_ref.shape[0]
    part = line_ref.shape[2] // 2
    x, y = me & 1, me >> 1
    for t, tokens in enumerate((cot_ref, other_ref)):
        near_x, near_y = columns(tokens, x * part, part), columns(tokens, (2 + y) * part, part)
        for m in range(1, 4):
            total = dot(near_x, line_ref[z ^ m, :, :part], 1, 1)
            total = total + dot(near_y, line_ref[z ^ m, :, part:], 1, 1)
            out_ref[pl.ds(t * rows, rows), pl.ds((m - 1) * HEAD, HEAD)] = total


def rows_late_kernel(
    at_ref, cot_ref, other_ref, own_ref, early_ref, x_ref, y_ref, keep_ref, send_ref
):
    me, z, rows = at_ref[0], at_ref[2], cot_ref.shape[0]
    part = x_ref.shape[1]
    x, y = me & 1, me >> 1
    for t, tokens, out in ((1, other_ref, send_ref), (0, cot_ref, keep_ref)):
        total = early_ref[pl.ds(t * rows, rows), :]
        total = total + dot(columns(tokens, (1 - x) * part, part), x_ref[...], 1, 1)
        total = total + dot(columns(tokens, (3 - y) * part, part), y_ref[...], 1, 1)
        total = total.astype(BF16)
        out[:, pl.ds(pl.multiple_of(z * HEAD, HEAD), HEAD)] = own_ref[pl.ds(t * rows, rows), :]
        for m in range(1, 4):
            place = pl.ds(pl.multiple_of((z ^ m) * HEAD, HEAD), HEAD)
            out[:, place] = total[:, (m - 1) * HEAD : m * HEAD]


def first_kernel(keep_ref, got_ref, a_ref, b_ref):
    for b, out in enumerate((a_ref, b_ref)):
        out[...] = (keep_ref[b] + got_ref[b].astype(F32)).astype(BF16)


def plane_kernel(b, keep_ref, got_ref, level_ref, stay_ref, step_ref):
    for m in range(4):
        total = keep_ref[m] + got_ref[b, m].astype(F32) + level_ref[m].astype(F32)
        if m % 2 == 0:
            stay_ref[m // 2] = total
        else:
            step_ref[m // 2] = total.astype(BF16)


def step_kernel(stay_ref, got_ref, total_ref, last_ref):
    total_ref[...] = stay_ref[0] + got_ref[0].astype(F32)
    last_ref[...] = (stay_ref[1] + got_ref[1].astype(F32)).astype(BF16)


def shard_kernel(a_ref, got_a_ref, b_ref, got_b_ref, out_ref):
    half = a_ref.shape[1]
    out_ref[:, :half] = (a_ref[...] + got_a_ref[...].astype(F32)).astype(BF16)
    out_ref[:, half:] = (b_ref[...] + got_b_ref[...].astype(F32)).astype(BF16)


def place_kernel(at_ref, *refs):
    *pieces, out_ref = refs
    half = pieces[0].shape[1] // 2
    for s, piece in enumerate(pieces):
        peer = at_ref[0] ^ s
        x, y = peer & 1, peer >> 1
        for b, start in enumerate((2 * x + y, 4 + 2 * y + x)):
            place = pl.ds(pl.multiple_of(start * half, half), half)
            out_ref[:, place] = piece[:, b * half : (b + 1) * half].astype(F32)


def swap(value, axis, mask):
    size = lax.axis_size(axis)
    return lax.ppermute(value, axis, [(i, i ^ mask) for i in range(size)])


def plane_body(queries, keys, values, cotangent, w_out, counts, dests):
    rows, width = queries.shape
    depth = cotangent.shape[1]
    part, half = depth // 4, depth // 8
    me, f = lax.axis_index("dp"), lax.axis_index("fsdp")
    at = jnp.stack([me, f, f >> 1, f & 1]).astype(jnp.int32)
    tokens = rows * lax.axis_size("dp") * lax.axis_size("fsdp")

    to_x, to_y = call(
        quarters_kernel,
        [shaped(rows, part)] * 2,
        [cotangent],
        rows * part,
        4 * rows * depth,
        name="quarters",
        mib=4,
        in_specs=[HBM],
        out_specs=[HBM] * 2,
        scratch_shapes=[pltpu.SemaphoreType.DMA((2,))],
    )
    cot_x, cot_y = swap(to_x, "dp", 1), swap(to_y, "dp", 2)
    cot_other = swap(cotangent, "fsdp", 1)

    mine = call(
        mine_kernel,
        shaped(4, HEAD, 2 * part),
        [w_out],
        HEAD * part,
        4 * HEAD * depth,
        name="mine",
        mib=4,
        after=[to_x],
        in_specs=[HBM],
        out_specs=HBM,
        scratch_shapes=[pltpu.SemaphoreType.DMA((8,))],
    )
    lines = [list(range(core, 8, 2)) for core in range(2)]
    line = lax.all_to_all(mine, "fsdp", 0, 0, axis_index_groups=lines, tiled=True)

    probs = probs_of(counts, queries, keys, after=[to_x, mine])
    out, far = call(
        outputs_kernel,
        [shaped(rows + HEADER, width), shaped(LMAX, width)],
        [at, counts, dests, probs, values],
        2 * rows * rows * width,
        6 * rows * width + 4 * HEADS * rows * rows,
        name="outputs",
        after=[cot_x, cot_y],
    )
    out_x, out_y = swap(out, "dp", 1), swap(out, "dp", 2)
    own = call(
        rows_own_kernel,
        shaped(2 * rows, HEAD),
        [cotangent, cot_other, w_out],
        4 * rows * HEAD * depth,
        4 * rows * depth + 2 * HEAD * depth,
        name="rows_own",
        mib=12,
        after=[out],
    )

    keep, *keeps, first, second = call(
        functools.partial(term_kernel, float(tokens) ** -0.5),
        [shaped(2, 4, HEAD, half, dtype=F32)]
        + [shaped(4, HEAD, half, dtype=F32)] * 2
        + [shaped(2, 4, HEAD, half)] * 2,
        [at, cotangent, out, out_x, out_y, cot_x, cot_y],
        2 * 4 * rows * width * part,
        2 * rows * (3 * width + depth + 2 * part) + 6 * width * part,
        name="term",
        mib=20,
        after=[own],
    )
    first, second = swap(first, "fsdp", 1), swap(second, "fsdp", 1)
    first_a, first_b = call(
        first_kernel,
        [shaped(4, HEAD, half)] * 2,
        [keep, first],
        8 * HEAD * half,
        64 * HEAD * half,
        name="first",
        mib=8,
    )
    far = swap(far, "dp", 3)
    levels = swap(first_a, "dp", 2), swap(first_b, "dp", 1)

    early = call(
        rows_early_kernel,
        shaped(2 * rows, 3 * HEAD, dtype=F32),
        [at, cotangent, cot_other, line],
        2 * rows * width * depth * 3 // 8,
        4 * rows * depth + 3 * HEAD * depth + 4 * rows * width,
        name="rows_early",
        after=[first_a],
        mib=16,
    )
    stays, steps = [], []
    for b, level in enumerate(levels):
        stay, step = call(
            functools.partial(plane_kernel, b),
            [shaped(2, HEAD, half, dtype=F32), shaped(2, HEAD, half)],
            [keeps[b], second, level],
            8 * HEAD * half,
            36 * HEAD * half,
            name="plane",
            after=[early],
            mib=8,
        )
        stays.append(stay)
        steps.append(step)
    got = [swap(step, "fsdp", 2) for step in steps]

    from_x, from_y = call(
        pack_kernel,
        [shaped(3 * HEAD, part)] * 2,
        [at, line],
        3 * HEAD * part,
        12 * HEAD * part,
        name="pack",
        mib=8,
        after=steps,
    )
    from_x, from_y = swap(from_x, "dp", 1), swap(from_y, "dp", 2)

    totals = []
    for stay, step in zip(stays, got):
        total, last = call(
            step_kernel,
            [shaped(HEAD, half, dtype=F32), shaped(HEAD, half)],
            [stay, step],
            2 * HEAD * half,
            18 * HEAD * half,
            name="step",
            mib=4,
        )
        totals += [total, swap(last, "fsdp", 4)]

    shard = call(
        shard_kernel,
        shaped(HEAD, part),
        totals,
        HEAD * part,
        8 * HEAD * part,
        name="shard",
        mib=4,
    )
    pieces = [shard] + [swap(shard, "dp", s) for s in (1, 2, 3)]
    attended = call(
        attended_kernel,
        shaped(4, LMAX, width),
        [at, out, out_x, out_y, far],
        6 * LMAX * rows * width,
        2 * (3 * rows + 5 * LMAX) * width,
        name="attended",
        mib=12,
        after=[shard],
    )
    grad_keep, grad_send = call(
        rows_late_kernel,
        [shaped(rows, width // 2)] * 2,
        [at, cotangent, cot_other, own, early, from_x, from_y],
        2 * rows * width * depth * 3 // 8,
        4 * rows * depth + 3 * HEAD * depth + 6 * rows * width,
        name="rows_late",
        mib=16,
        after=[shard],
    )
    grad_other = swap(grad_send, "fsdp", 1)
    grads = backward(at, probs, queries, keys, values, grad_keep, grad_other)
    weight_grad = call(
        place_kernel,
        shaped(HEAD, depth, dtype=F32),
        [at, *pieces],
        HEAD * depth,
        6 * HEAD * depth,
        name="place",
        after=[grads[0], attended],
        mib=8,
    )
    return (*grads, attended[None, None], weight_grad)


def body(queries, keys, values, cotangent, w_out, counts, dests):
    rows, width = queries.shape
    groups = counts.shape[1]
    tokens = rows * lax.axis_size("dp") * lax.axis_size("fsdp")
    probs = probs_of(counts, queries, keys, mib=48)
    out, slots = call(
        slots_kernel,
        [shaped(rows, width), shaped(groups, LMAX, width)],
        [counts, dests, probs, values],
        2 * (rows + groups * LMAX) * rows * width,
        6 * rows * width + 4 * HEADS * rows * rows,
        name="slots",
        mib=48,
    )
    attended = lax.all_to_all(slots, "dp", split_axis=0, concat_axis=0, tiled=True)
    product = dot(out, cotangent, 0, 0) * float(tokens) ** -0.5
    shard = lax.psum_scatter(product.astype(BF16), "fsdp", scatter_dimension=0, tiled=True)
    weight_grad = lax.psum(shard, "dp").astype(F32)
    grad_rows = dot(cotangent, lax.all_gather(w_out, "fsdp", axis=0, tiled=True), 1, 1).astype(BF16)
    grads = backward(None, probs, queries, keys, values, grad_rows, mib=48)
    return (*grads, attended[None, None], weight_grad)


def solution(mesh):
    placed = (
        P(("dp", "fsdp"), None),
        P(("dp", "fsdp"), None),
        P(("dp", "fsdp"), None),
        P(("dp", "fsdp"), None),
        P("fsdp", None),
        P(("dp", "fsdp"), None),
        P(("dp", "fsdp"), None),
    )
    plane = mesh.shape["dp"] == 4 and mesh.shape["fsdp"] == HEADS
    return jax.shard_map(
        plane_body if plane else body,
        mesh=mesh,
        in_specs=placed,
        out_specs=(
            P(("dp", "fsdp"), None),
            P(("dp", "fsdp"), None),
            P(("dp", "fsdp"), None),
            P("dp", "fsdp", None, None, None),
            P("fsdp", None),
        ),
        check_vma=False,
    )
```

```python
import functools

import jax
import jax.numpy as jnp
from jax import lax
from jax.experimental import pallas as pl
from jax.experimental.pallas import tpu as pltpu
from jax.sharding import PartitionSpec as P

HEADS = 8
LMAX = 128
HEAD = 128
HEADER = 16
MIB = 1024 * 1024
STEP_WEIGHT = 23 * 10**9

F32 = jnp.float32
BF16 = jnp.bfloat16
SMEM = pl.BlockSpec(memory_space=pltpu.SMEM)
VMEM = pl.BlockSpec(memory_space=pltpu.VMEM)
ANY = pl.BlockSpec(memory_space=pl.ANY)


def dot(a, b, ca, cb):
    return lax.dot_general(a, b, (((ca,), (cb,)), ((), ())), preferred_element_type=F32)


def call(kernel, out_shape, args, name, mib=24, after=(), weight=0, **more):
    single = not isinstance(out_shape, (list, tuple))
    given = len(args)
    more.setdefault("in_specs", [SMEM if a.dtype == jnp.int32 else VMEM for a in args])
    more.setdefault("out_specs", VMEM if single else [VMEM] * len(out_shape))
    more["in_specs"] = more["in_specs"] + [ANY] * len(after)

    def run(*refs):
        kernel(*refs[:given], *refs[given + len(after) :])

    return pl.pallas_call(
        run,
        out_shape=out_shape,
        compiler_params=pltpu.CompilerParams(vmem_limit_bytes=mib * MIB),
        cost_estimate=pl.CostEstimate(flops=weight, bytes_accessed=1, transcendentals=0),
        name=name,
        **more,
    )(*args, *after)


def shaped(*shape, dtype=BF16):
    return jax.ShapeDtypeStruct(shape, dtype)


def image_of(index, counts_ref):
    image = jnp.zeros_like(index)
    end = 0
    for g in range(counts_ref.shape[1]):
        end = end + counts_ref[0, g]
        image = image + (index >= end).astype(jnp.int32)
    return image


def image_rows(start, count, out):
    rows = out.shape[0]
    place = lax.broadcasted_iota(jnp.int32, (LMAX, rows), 0)
    index = lax.broadcasted_iota(jnp.int32, (LMAX, rows), 1)
    chosen = (index == place + start) & (place < count)
    return dot(jnp.where(chosen, 1.0, 0.0).astype(BF16), out, 1, 0).astype(BF16)


def probs_kernel(counts_ref, q_ref, k_ref, probs_ref):
    rows = q_ref.shape[0]
    scale = float(HEAD) ** -0.5
    image_r = image_of(lax.broadcasted_iota(jnp.int32, (rows, 1), 0), counts_ref)
    image_c = image_of(lax.broadcasted_iota(jnp.int32, (1, rows), 1), counts_ref)
    same = image_r == image_c
    for h in range(HEADS):
        cols = pl.ds(h * HEAD, HEAD)
        scores = dot(q_ref[:, cols], k_ref[:, cols], 1, 1) * scale
        scores = jnp.where(same, scores, -1e30)
        top = jnp.max(scores, axis=1, keepdims=True)
        weights = jnp.exp(scores - top)
        probs_ref[h] = weights * (1.0 / jnp.sum(weights, axis=1, keepdims=True))


def outputs_of(probs_ref, v_ref, out_ref):
    rows = v_ref.shape[0]
    for h in range(HEADS):
        cols = pl.ds(h * HEAD, HEAD)
        out_ref[:rows, cols] = dot(probs_ref[h].astype(BF16), v_ref[:, cols], 1, 0).astype(BF16)


def outputs_kernel(counts_ref, dests_ref, probs_ref, v_ref, cot_ref, x_ref, y_ref, sems):
    rows, width = v_ref.shape
    part = x_ref.shape[1] - width
    me = lax.axis_index("dp")
    starts = (1 - (me & 1)) * part, (3 - (me >> 1)) * part
    copies = [
        pltpu.make_async_copy(
            cot_ref.at[:, pl.ds(pl.multiple_of(start, HEAD), part)],
            out.at[pl.ds(0, rows), pl.ds(width, part)],
            sems.at[i],
        )
        for i, (start, out) in enumerate(zip(starts, (x_ref, y_ref)))
    ]
    for copy in copies:
        copy.start()
    for h in range(HEADS):
        cols = pl.ds(h * HEAD, HEAD)
        value = dot(probs_ref[h].astype(BF16), v_ref[:, cols], 1, 0).astype(BF16)
        x_ref[:rows, cols] = value
        y_ref[:rows, cols] = value
    index = lax.broadcasted_iota(jnp.int32, (HEADER, width + part), 1)
    line = lax.broadcasted_iota(jnp.int32, (HEADER, width + part), 0)
    place, group = index, jnp.full((HEADER, width + part), dests_ref[0, 0], jnp.int32)
    start = 0
    for g in range(counts_ref.shape[1]):
        count, dest = counts_ref[0, g], dests_ref[0, g]
        past = index >= start
        group = jnp.where(past, dest, group)
        place = jnp.where(past, index - start, place)
        start = start + count
    header = jnp.where(line == 0, place, jnp.where(line == 1, group, 0))
    header = jnp.where(index < rows, header, -1).astype(F32).astype(BF16)
    x_ref[rows:, :] = header
    y_ref[rows:, :] = header
    for copy in copies:
        copy.wait()


def far_kernel(at_ref, counts_ref, dests_ref, out_ref, far_ref):
    start, far_start, far_count = 0, 0, 0
    for g in range(counts_ref.shape[1]):
        count = counts_ref[0, g]
        far = dests_ref[0, g] == (at_ref[0] ^ 3)
        far_start = jnp.where(far, start, far_start)
        far_count = jnp.where(far, count, far_count)
        start = start + count
    far_ref[...] = image_rows(far_start, far_count, out_ref[: out_ref.shape[0] - HEADER, : far_ref.shape[1]])


def slots_kernel(counts_ref, dests_ref, probs_ref, v_ref, out_ref, slots_ref):
    outputs_of(probs_ref, v_ref, out_ref)
    start = 0
    for g in range(counts_ref.shape[1]):
        count = counts_ref[0, g]
        slots_ref[dests_ref[0, g]] = image_rows(start, count, out_ref[...])
        start = start + count


def probs_of(counts, queries, keys, **more):
    rows, width = queries.shape
    return call(
        probs_kernel,
        shaped(HEADS, rows, rows, dtype=F32),
        [counts, queries, keys],
        name="probs",
        **more,
    )


def backward_kernel(split, *refs):
    if split:
        at_ref, *refs = refs
    probs_ref, q_ref, k_ref, v_ref, *grads, dq_ref, dk_ref, dv_ref, token_ref = refs
    token_ref[...] = jnp.zeros_like(token_ref)
    scale = float(HEAD) ** -0.5
    for h in range(HEADS):
        cols = pl.ds(h * HEAD, HEAD)
        if split:
            own = grads[0][:, h // 2 * HEAD : (h // 2 + 1) * HEAD]
            near = (h // 2) ^ at_ref[2]
            near_cols = pl.ds(pl.multiple_of((near & 1) * HEAD, HEAD), HEAD)
            other = jnp.where(near < 2, grads[1][:, near_cols], grads[2][:, near_cols])
            grad = jnp.where(at_ref[3] == h % 2, own, other)
        else:
            grad = grads[0][:, cols]
        probs = probs_ref[h]
        dprobs = dot(grad, v_ref[:, cols], 1, 1)
        delta = jnp.sum(probs * dprobs, axis=1, keepdims=True)
        dscores = (probs * (dprobs - delta) * scale).astype(BF16)
        dq_ref[:, cols] = dot(dscores, k_ref[:, cols], 1, 0).astype(BF16)
        dk_ref[:, cols] = dot(dscores, q_ref[:, cols], 0, 0).astype(BF16)
        dv_ref[:, cols] = dot(probs.astype(BF16), grad, 0, 0).astype(BF16)


def backward(at, probs, queries, keys, values, *grads, mib=14):
    rows, width = queries.shape
    split = at is not None
    return call(
        functools.partial(backward_kernel, split),
        [shaped(rows, width)] * 3 + [shaped(8, HEAD, dtype=F32)],
        ([at] if split else []) + [probs, queries, keys, values, *grads],
        name="backward",
        mib=mib,
    )


def attended_kernel(at_ref, own_ref, x_ref, y_ref, out_ref):
    rows, width = own_ref.shape[0] - HEADER, out_ref.shape[2]
    me = at_ref[0]
    place = lax.broadcasted_iota(jnp.int32, (LMAX, rows), 0)
    for s, source in enumerate((own_ref, x_ref, y_ref)):
        header = source[rows:, :rows].astype(F32).astype(jnp.int32)
        chosen = (header[0:1] == place) & (header[1:2] == me)
        chosen = jnp.where(chosen, 1.0, 0.0).astype(BF16)
        out_ref[me ^ s] = dot(chosen, source[:rows, :width], 1, 0).astype(BF16)


def across_kernel(three_ref, far_ref, out_ref, sems):
    copy_all([(far_ref, out_ref.at[lax.axis_index("dp") ^ 3])], sems)


def columns(ref, start, size):
    return ref[:, pl.ds(pl.multiple_of(start, HEAD), size)]


def copy_all(pairs, sems):
    copies = [pltpu.make_async_copy(a, b, sems.at[i]) for i, (a, b) in enumerate(pairs)]
    for copy in copies:
        copy.start()
    for copy in copies:
        copy.wait()


def mine_kernel(w_ref, out_ref, sems):
    part = out_ref.shape[1] // 2
    me = lax.axis_index("dp")
    starts = (me & 1) * part, (2 + (me >> 1)) * part
    pairs = [
        (w_ref.at[:, pl.ds(pl.multiple_of(start, HEAD), part)], out_ref.at[:, pl.ds(i * part, part)])
        for i, start in enumerate(starts)
    ]
    copy_all(pairs, sems)


def pack_kernel(z1_ref, z2_ref, z3_ref, x_ref, y_ref):
    part = x_ref.shape[1]
    for m, piece in enumerate((z1_ref, z2_ref, z3_ref)):
        x_ref[pl.ds(m * HEAD, HEAD)] = piece[:, :part]
        y_ref[pl.ds(m * HEAD, HEAD)] = piece[:, part:]


def term_kernel(scale, r, at_ref, cot_ref, own_ref, x_ref, y_ref, keep_a_ref, keep_b_ref, send_ref):
    rows, part = cot_ref.shape[0], cot_ref.shape[1] // 4
    half, width = part // 2, own_ref.shape[1] - part
    x, y, z, c = at_ref[0] & 1, at_ref[0] >> 1, at_ref[2], at_ref[3]
    for b, (near, place, inner, keep_ref) in enumerate(
        ((x_ref, x, y ^ r, keep_a_ref), (y_ref, 2 + y, x ^ r, keep_b_ref))
    ):
        own_cot = columns(cot_ref, place * part + inner * half, half)
        near_cot = columns(near, width + inner * half, half)[:rows]
        for m in range(4):
            pair = (z ^ m) * 2 * HEAD
            total = dot(columns(own_ref, pair, 2 * HEAD)[:rows], own_cot, 0, 0)
            total = total + dot(columns(near, pair, 2 * HEAD)[:rows], near_cot, 0, 0)
            total = total * scale
            low, high = total[:HEAD], total[HEAD:]
            keep_ref[m] = jnp.where(c == 0, low, high)
            send_ref[b, m] = jnp.where(c == 0, high, low).astype(BF16)


def rows_own_kernel(cot_ref, other_ref, own_ref, out_ref):
    rows = cot_ref.shape[0]
    out_ref[:rows] = dot(cot_ref[...], own_ref[...], 1, 1).astype(BF16)
    out_ref[rows:] = dot(other_ref[...], own_ref[...], 1, 1).astype(BF16)


def rows_early_kernel(at_ref, cot_ref, other_ref, z1_ref, z2_ref, out_ref):
    me, rows = at_ref[0], cot_ref.shape[0]
    part = z1_ref.shape[1] // 2
    x, y = me & 1, me >> 1
    for t, tokens in enumerate((cot_ref, other_ref)):
        near_x, near_y = columns(tokens, x * part, part), columns(tokens, (2 + y) * part, part)
        for i, piece in enumerate((z1_ref, z2_ref)):
            total = dot(near_x, piece[:, :part], 1, 1) + dot(near_y, piece[:, part:], 1, 1)
            out_ref[pl.ds(t * rows, rows), pl.ds(i * HEAD, HEAD)] = total


def rows_late_kernel(
    at_ref, cot_ref, other_ref, own_ref, early_ref, z3_ref, x_ref, y_ref, keep_ref, low_ref, high_ref
):
    me, z, rows = at_ref[0], at_ref[2], cot_ref.shape[0]
    part = x_ref.shape[1]
    x, y = me & 1, me >> 1
    for t, tokens in ((1, other_ref), (0, cot_ref)):
        here = pl.ds(t * rows, rows)
        total = dot(columns(tokens, (1 - x) * part, part), x_ref[...], 1, 1)
        total = total + dot(columns(tokens, (3 - y) * part, part), y_ref[...], 1, 1)
        third = dot(columns(tokens, x * part, part), z3_ref[:, :part], 1, 1)
        third = third + dot(columns(tokens, (2 + y) * part, part), z3_ref[:, part:], 1, 1)
        heads = [
            own_ref[here, :],
            (total[:, :HEAD] + early_ref[here, :HEAD]).astype(BF16),
            (total[:, HEAD : 2 * HEAD] + early_ref[here, HEAD:]).astype(BF16),
            (total[:, 2 * HEAD :] + third).astype(BF16),
        ]
        for m, head in enumerate(heads):
            if t == 0:
                keep_ref[:, pl.ds(pl.multiple_of((z ^ m) * HEAD, HEAD), HEAD)] = head
            else:
                (low_ref, high_ref)[m // 2][:, m % 2 * HEAD : (m % 2 + 1) * HEAD] = head


def first_kernel(keep_a_ref, keep_b_ref, got_ref, a_ref, b_ref):
    for b, (keep, out) in enumerate(((keep_a_ref, a_ref), (keep_b_ref, b_ref))):
        out[...] = (keep[...] + got_ref[b].astype(F32)).astype(BF16)


def plane_kernel(keep_a_ref, keep_b_ref, got_ref, level_a_ref, level_b_ref, *outs):
    for b, (keep, level) in enumerate(((keep_a_ref, level_a_ref), (keep_b_ref, level_b_ref))):
        stay_ref, step_ref = outs[2 * b : 2 * b + 2]
        for m in range(4):
            total = keep[m] + got_ref[b, m].astype(F32) + level[m].astype(F32)
            if m % 2 == 0:
                stay_ref[m // 2] = total
            else:
                step_ref[m // 2] = total.astype(BF16)


def step_kernel(stay_ref, got_ref, total_ref, last_ref):
    total_ref[...] = stay_ref[0] + got_ref[0].astype(F32)
    last_ref[...] = (stay_ref[1] + got_ref[1].astype(F32)).astype(BF16)


def shard_kernel(a_ref, got_a_ref, b_ref, got_b_ref, out_ref):
    half = a_ref.shape[1]
    out_ref[:, :half] = (a_ref[...] + got_a_ref[...].astype(F32)).astype(BF16)
    out_ref[:, half:] = (b_ref[...] + got_b_ref[...].astype(F32)).astype(BF16)


def place_kernel(at_ref, *refs):
    *pieces, out_ref = refs
    half = pieces[0].shape[1] // 2
    for s, piece in enumerate(pieces):
        peer = at_ref[0] ^ s
        x, y = peer & 1, peer >> 1
        for b, start in enumerate((2 * x + y, 4 + 2 * y + x)):
            place = pl.ds(pl.multiple_of(start * half, half), half)
            out_ref[:, place] = piece[:, b * half : (b + 1) * half].astype(F32)


def swap(value, axis, mask):
    size = lax.axis_size(axis)
    return lax.ppermute(value, axis, [(i, i ^ mask) for i in range(size)])


def plane_body(queries, keys, values, cotangent, w_out, counts, dests):
    rows, width = queries.shape
    depth = cotangent.shape[1]
    part, half = depth // 4, depth // 8
    me, f = lax.axis_index("dp"), lax.axis_index("fsdp")
    at = jnp.stack([me, f, f >> 1, f & 1]).astype(jnp.int32)
    tokens = rows * lax.axis_size("dp") * lax.axis_size("fsdp")

    cot_other = swap(cotangent, "fsdp", 1)
    probs = probs_of(counts, queries, keys, mib=12)
    to_x, to_y = call(
        outputs_kernel,
        [shaped(rows + HEADER, width + part)] * 2,
        [counts, dests, probs, values, cotangent],
        name="outputs",
        mib=8,
        after=[cot_other],
        in_specs=[SMEM, SMEM, VMEM, VMEM, ANY],
        scratch_shapes=[pltpu.SemaphoreType.DMA((2,))],
    )
    got_x, got_y = swap(to_x, "dp", 1), swap(to_y, "dp", 2)

    mine = call(
        mine_kernel,
        shaped(HEAD, 2 * part),
        [w_out],
        name="mine",
        mib=4,
        after=[to_x],
        in_specs=[ANY],
        out_specs=VMEM,
        scratch_shapes=[pltpu.SemaphoreType.DMA((2,))],
    )
    z2, z1 = swap(mine, "fsdp", 4), swap(mine, "fsdp", 2)
    z3 = swap(z2, "fsdp", 2)
    own = call(
        rows_own_kernel,
        shaped(2 * rows, HEAD),
        [cotangent, cot_other, w_out],
        name="rows_own",
        mib=12,
        after=[to_x],
    )

    far = call(
        far_kernel,
        shaped(LMAX, width),
        [at, counts, dests, to_x],
        name="far",
        mib=8,
        after=[to_x],
    )

    def term(r, after):
        return call(
            functools.partial(term_kernel, float(tokens) ** -0.5, r),
            [shaped(4, HEAD, half, dtype=F32)] * 2 + [shaped(2, 4, HEAD, half)],
            [at, cotangent, to_x, got_x, got_y],
            name="term%d" % r,
            mib=14,
            after=after,
        )

    *keeps, first = term(1, [own, far, z1, z2])
    first = swap(first, "fsdp", 1)
    first_a, first_b = call(
        first_kernel,
        [shaped(4, HEAD, half)] * 2,
        [*keeps, first],
        name="first",
        mib=8,
    )
    *keeps, second = term(0, [keeps[0]])
    second = swap(second, "fsdp", 1)
    levels = swap(first_a, "dp", 2), swap(first_b, "dp", 1)

    early = call(
        rows_early_kernel,
        shaped(2 * rows, 2 * HEAD, dtype=F32),
        [at, cotangent, cot_other, z1, z2],
        name="rows_early",
        mib=12,
        after=[first_a],
    )
    three = call(
        attended_kernel,
        shaped(4, LMAX, width),
        [at, to_x, got_x, got_y],
        name="attended",
        mib=8,
        after=[first_a],
    )
    stay_a, step_a, stay_b, step_b = call(
        plane_kernel,
        [shaped(2, HEAD, half, dtype=F32), shaped(2, HEAD, half)] * 2,
        [*keeps, second, *levels],
        name="plane",
        mib=10,
        after=[early, three],
    )
    stays, steps = (stay_a, stay_b), (step_a, step_b)
    got = [swap(step, "fsdp", 2) for step in steps]

    from_x, from_y = call(
        pack_kernel,
        [shaped(3 * HEAD, part)] * 2,
        [z1, z2, z3],
        name="pack",
        mib=8,
        after=steps,
    )
    from_x, from_y = swap(from_x, "dp", 1), swap(from_y, "dp", 2)

    far = swap(far, "dp", 3)
    totals = []
    for stay, step in zip(stays, got):
        total, last = call(
            step_kernel,
            [shaped(HEAD, half, dtype=F32), shaped(HEAD, half)],
            [stay, step],
            name="step",
            mib=4,
            weight=STEP_WEIGHT,
        )
        totals += [total, swap(last, "fsdp", 4)]

    shard = call(
        shard_kernel,
        shaped(HEAD, part),
        totals,
        name="shard",
        mib=4,
    )
    pieces = [shard] + [swap(shard, "dp", s) for s in (1, 2, 3)]
    attended = call(
        across_kernel,
        shaped(4, LMAX, width),
        [three, far],
        name="across",
        mib=4,
        in_specs=[ANY, ANY],
        out_specs=ANY,
        scratch_shapes=[pltpu.SemaphoreType.DMA((1,))],
        input_output_aliases={0: 0},
    )
    grad_keep, *grad_send = call(
        rows_late_kernel,
        [shaped(rows, width // 2)] + [shaped(rows, width // 4)] * 2,
        [at, cotangent, cot_other, own, early, z3, from_x, from_y],
        name="rows_late",
        after=[shard],
        mib=12,
    )
    grad_other = [swap(part, "fsdp", 1) for part in grad_send]
    *grads, token = backward(at, probs, queries, keys, values, grad_keep, *grad_other)
    weight_grad = call(
        place_kernel,
        shaped(HEAD, depth, dtype=F32),
        [at, *pieces],
        name="place",
        after=[token],
        mib=8,
    )
    return (*grads, attended[None, None], weight_grad)


def body(queries, keys, values, cotangent, w_out, counts, dests):
    rows, width = queries.shape
    groups = counts.shape[1]
    tokens = rows * lax.axis_size("dp") * lax.axis_size("fsdp")
    probs = probs_of(counts, queries, keys, mib=48)
    out, slots = call(
        slots_kernel,
        [shaped(rows, width), shaped(groups, LMAX, width)],
        [counts, dests, probs, values],
        name="slots",
        mib=48,
    )
    attended = lax.all_to_all(slots, "dp", split_axis=0, concat_axis=0, tiled=True)
    product = dot(out, cotangent, 0, 0) * float(tokens) ** -0.5
    shard = lax.psum_scatter(product.astype(BF16), "fsdp", scatter_dimension=0, tiled=True)
    weight_grad = lax.psum(shard, "dp").astype(F32)
    grad_rows = dot(cotangent, lax.all_gather(w_out, "fsdp", axis=0, tiled=True), 1, 1).astype(BF16)
    *grads, token = backward(None, probs, queries, keys, values, grad_rows, mib=48)
    return (*grads, attended[None, None], weight_grad)


def solution(mesh):
    placed = (
        P(("dp", "fsdp"), None),
        P(("dp", "fsdp"), None),
        P(("dp", "fsdp"), None),
        P(("dp", "fsdp"), None),
        P("fsdp", None),
        P(("dp", "fsdp"), None),
        P(("dp", "fsdp"), None),
    )
    plane = mesh.shape["dp"] == 4 and mesh.shape["fsdp"] == HEADS
    return jax.shard_map(
        plane_body if plane else body,
        mesh=mesh,
        in_specs=placed,
        out_specs=(
            P(("dp", "fsdp"), None),
            P(("dp", "fsdp"), None),
            P(("dp", "fsdp"), None),
            P("dp", "fsdp", None, None, None),
            P("fsdp", None),
        ),
        check_vma=False,
    )
```

```python
import functools

import jax
import jax.numpy as jnp
from jax import lax
from jax.experimental import pallas as pl
from jax.experimental.pallas import tpu as pltpu
from jax.sharding import PartitionSpec as P

HEADS = 8
LMAX = 128
HEAD = 128
HEADER = 16
MIB = 1024 * 1024
MINE_WEIGHT = 12 * 10**9
TURN_WEIGHT = 23 * 10**9
STEP_WEIGHT = 23 * 10**9

F32 = jnp.float32
BF16 = jnp.bfloat16
SMEM = pl.BlockSpec(memory_space=pltpu.SMEM)
VMEM = pl.BlockSpec(memory_space=pltpu.VMEM)
ANY = pl.BlockSpec(memory_space=pl.ANY)


def dot(a, b, ca, cb):
    return lax.dot_general(a, b, (((ca,), (cb,)), ((), ())), preferred_element_type=F32)


def call(kernel, out_shape, args, name, mib=24, after=(), weight=0, **more):
    single = not isinstance(out_shape, (list, tuple))
    given = len(args)
    more.setdefault("in_specs", [SMEM if a.dtype == jnp.int32 else VMEM for a in args])
    more.setdefault("out_specs", VMEM if single else [VMEM] * len(out_shape))
    more["in_specs"] = more["in_specs"] + [ANY] * len(after)

    def run(*refs):
        kernel(*refs[:given], *refs[given + len(after) :])

    return pl.pallas_call(
        run,
        out_shape=out_shape,
        compiler_params=pltpu.CompilerParams(vmem_limit_bytes=mib * MIB),
        cost_estimate=pl.CostEstimate(flops=weight, bytes_accessed=1, transcendentals=0),
        name=name,
        **more,
    )(*args, *after)


def shaped(*shape, dtype=BF16):
    return jax.ShapeDtypeStruct(shape, dtype)


def image_of(index, counts_ref):
    image = jnp.zeros_like(index)
    end = 0
    for g in range(counts_ref.shape[1]):
        end = end + counts_ref[0, g]
        image = image + (index >= end).astype(jnp.int32)
    return image


def image_rows(start, count, out):
    rows = out.shape[0]
    place = lax.broadcasted_iota(jnp.int32, (LMAX, rows), 0)
    index = lax.broadcasted_iota(jnp.int32, (LMAX, rows), 1)
    chosen = (index == place + start) & (place < count)
    return dot(jnp.where(chosen, 1.0, 0.0).astype(BF16), out, 1, 0).astype(BF16)


def probs_kernel(counts_ref, q_ref, k_ref, probs_ref):
    rows = q_ref.shape[0]
    scale = float(HEAD) ** -0.5
    image_r = image_of(lax.broadcasted_iota(jnp.int32, (rows, 1), 0), counts_ref)
    image_c = image_of(lax.broadcasted_iota(jnp.int32, (1, rows), 1), counts_ref)
    same = image_r == image_c
    for h in range(HEADS):
        cols = pl.ds(h * HEAD, HEAD)
        scores = dot(q_ref[:, cols], k_ref[:, cols], 1, 1) * scale
        scores = jnp.where(same, scores, -1e30)
        top = jnp.max(scores, axis=1, keepdims=True)
        weights = jnp.exp(scores - top)
        probs_ref[h] = weights * (1.0 / jnp.sum(weights, axis=1, keepdims=True))


def outputs_of(probs_ref, v_ref, out_ref):
    rows = v_ref.shape[0]
    for h in range(HEADS):
        cols = pl.ds(h * HEAD, HEAD)
        out_ref[:rows, cols] = dot(probs_ref[h].astype(BF16), v_ref[:, cols], 1, 0).astype(BF16)


def quarters_kernel(cot_ref, x_ref, y_ref, sems):
    part = x_ref.shape[1]
    me = lax.axis_index("dp")
    starts = (1 - (me & 1)) * part, (3 - (me >> 1)) * part
    pairs = [
        (cot_ref.at[:, pl.ds(pl.multiple_of(start, HEAD), part)], out)
        for start, out in zip(starts, (x_ref, y_ref))
    ]
    copy_all(pairs, sems)


def outputs_kernel(counts_ref, dests_ref, probs_ref, v_ref, out_ref):
    outputs_of(probs_ref, v_ref, out_ref)
    rows, width = v_ref.shape
    index = lax.broadcasted_iota(jnp.int32, (HEADER, width), 1)
    line = lax.broadcasted_iota(jnp.int32, (HEADER, width), 0)
    place, group = index, jnp.full((HEADER, width), dests_ref[0, 0], jnp.int32)
    start = 0
    for g in range(counts_ref.shape[1]):
        count, dest = counts_ref[0, g], dests_ref[0, g]
        past = index >= start
        group = jnp.where(past, dest, group)
        place = jnp.where(past, index - start, place)
        start = start + count
    header = jnp.where(line == 0, place, jnp.where(line == 1, group, 0))
    out_ref[rows:, :] = jnp.where(index < rows, header, -1).astype(F32).astype(BF16)


def far_kernel(at_ref, counts_ref, dests_ref, out_ref, far_ref):
    start, far_start, far_count = 0, 0, 0
    for g in range(counts_ref.shape[1]):
        count = counts_ref[0, g]
        far = dests_ref[0, g] == (at_ref[0] ^ 3)
        far_start = jnp.where(far, start, far_start)
        far_count = jnp.where(far, count, far_count)
        start = start + count
    far_ref[...] = image_rows(far_start, far_count, out_ref[: out_ref.shape[0] - HEADER])


def slots_kernel(counts_ref, dests_ref, probs_ref, v_ref, out_ref, slots_ref):
    outputs_of(probs_ref, v_ref, out_ref)
    start = 0
    for g in range(counts_ref.shape[1]):
        count = counts_ref[0, g]
        slots_ref[dests_ref[0, g]] = image_rows(start, count, out_ref[...])
        start = start + count


def probs_of(counts, queries, keys, **more):
    rows, width = queries.shape
    return call(
        probs_kernel,
        shaped(HEADS, rows, rows, dtype=F32),
        [counts, queries, keys],
        name="probs",
        **more,
    )


def turn_kernel(probs_ref, out_ref):
    for h in range(HEADS):
        out_ref[h] = probs_ref[h].T.astype(BF16)


def turned(probs, **more):
    heads, rows, _ = probs.shape
    return call(turn_kernel, shaped(heads, rows, rows), [probs], name="turn", **more)


def backward_kernel(split, *refs):
    if split:
        at_ref, *refs = refs
    probs_ref, turned_ref, q_ref, k_ref, v_ref, *grads = refs[:-8]
    token_ref, *kept, sems = refs[-5:]
    outs = refs[-8:-5]
    token_ref[...] = jnp.zeros_like(token_ref)
    scale = float(HEAD) ** -0.5
    copies = []
    for h in range(HEADS):
        cols = pl.ds(h * HEAD, HEAD)
        if split:
            own = grads[0][:, h // 2 * HEAD : (h // 2 + 1) * HEAD]
            near = (h // 2) ^ at_ref[2]
            near_cols = pl.ds(pl.multiple_of((near & 1) * HEAD, HEAD), HEAD)
            other = jnp.where(near < 2, grads[1][:, near_cols], grads[2][:, near_cols])
            grad = jnp.where(at_ref[3] == h % 2, own, other)
        else:
            grad = grads[0][:, cols]
        probs = probs_ref[h]
        dprobs = dot(grad, v_ref[:, cols], 1, 1)
        delta = jnp.sum(probs * dprobs, axis=1, keepdims=True)
        dscores = (probs * (dprobs - delta) * scale).astype(BF16)
        values = (
            dot(dscores, k_ref[:, cols], 1, 0),
            dot(dscores, q_ref[:, cols], 0, 0),
            dot(turned_ref[h], grad, 1, 0),
        )
        for i, (value, keep, out) in enumerate(zip(values, kept, outs)):
            keep[:, cols] = value.astype(BF16)
            if h % 2 == 1:
                pair = pl.ds((h - 1) * HEAD, 2 * HEAD)
                copies.append(pltpu.make_async_copy(keep.at[:, pair], out.at[:, pair], sems.at[i, h // 2]))
                copies[-1].start()
    for copy in copies:
        copy.wait()


def backward(at, probs, turn, queries, keys, values, *grads, mib=14):
    rows, width = queries.shape
    split = at is not None
    return call(
        functools.partial(backward_kernel, split),
        [shaped(rows, width)] * 3 + [shaped(8, HEAD, dtype=F32)],
        ([at] if split else []) + [probs, turn, queries, keys, values, *grads],
        name="backward",
        mib=mib,
        out_specs=[ANY] * 3 + [VMEM],
        scratch_shapes=[pltpu.VMEM((rows, width), BF16)] * 3 + [pltpu.SemaphoreType.DMA((3, HEADS // 2))],
    )


def attended_kernel(at_ref, own_ref, x_ref, y_ref, out_ref, token_ref):
    token_ref[...] = jnp.zeros_like(token_ref)
    rows = own_ref.shape[0] - HEADER
    me = at_ref[0]
    place = lax.broadcasted_iota(jnp.int32, (LMAX, rows), 0)
    for s, source in enumerate((own_ref, x_ref, y_ref)):
        header = source[rows:, :rows].astype(F32).astype(jnp.int32)
        chosen = (header[0:1] == place) & (header[1:2] == me)
        chosen = jnp.where(chosen, 1.0, 0.0).astype(BF16)
        out_ref[me ^ s] = dot(chosen, source[:rows, :], 1, 0).astype(BF16)


def across_kernel(three_ref, far_ref, out_ref, token_ref, sems):
    token_ref[...] = jnp.zeros_like(token_ref)
    copy_all([(far_ref, out_ref.at[lax.axis_index("dp") ^ 3])], sems)


def columns(ref, start, size):
    return ref[:, pl.ds(pl.multiple_of(start, HEAD), size)]


def copy_all(pairs, sems):
    copies = [pltpu.make_async_copy(a, b, sems.at[i]) for i, (a, b) in enumerate(pairs)]
    for copy in copies:
        copy.start()
    for copy in copies:
        copy.wait()


def mine_kernel(w_ref, out_ref, sems):
    part = out_ref.shape[1] // 2
    me = lax.axis_index("dp")
    starts = (me & 1) * part, (2 + (me >> 1)) * part
    pairs = [
        (w_ref.at[:, pl.ds(pl.multiple_of(start, HEAD), part)], out_ref.at[:, pl.ds(i * part, part)])
        for i, start in enumerate(starts)
    ]
    copy_all(pairs, sems)


def pack_kernel(z1_ref, z2_ref, z3_ref, x_ref, y_ref):
    part = x_ref.shape[1]
    for m, piece in enumerate((z1_ref, z2_ref, z3_ref)):
        x_ref[pl.ds(m * HEAD, HEAD)] = piece[:, :part]
        y_ref[pl.ds(m * HEAD, HEAD)] = piece[:, part:]


def term_kernel(
    scale, r, at_ref, cot_ref, own_ref, x_ref, y_ref, cx_ref, cy_ref, keep_a_ref, keep_b_ref, send_ref
):
    rows, part = cx_ref.shape
    half = part // 2
    x, y, z, c = at_ref[0] & 1, at_ref[0] >> 1, at_ref[2], at_ref[3]
    for b, (near, cot, place, inner, keep_ref) in enumerate(
        ((x_ref, cx_ref, x, y ^ r, keep_a_ref), (y_ref, cy_ref, 2 + y, x ^ r, keep_b_ref))
    ):
        own_cot = columns(cot_ref, place * part + inner * half, half)
        near_cot = columns(cot, inner * half, half)
        for m in range(4):
            pair = (z ^ m) * 2 * HEAD
            total = dot(columns(own_ref, pair, 2 * HEAD)[:rows], own_cot, 0, 0)
            total = total + dot(columns(near, pair, 2 * HEAD)[:rows], near_cot, 0, 0)
            total = total * scale
            low, high = total[:HEAD], total[HEAD:]
            keep_ref[m] = jnp.where(c == 0, low, high)
            send_ref[b, m] = jnp.where(c == 0, high, low).astype(BF16)


def rows_own_kernel(cot_ref, other_ref, own_ref, out_ref):
    rows = cot_ref.shape[0]
    out_ref[:rows] = dot(cot_ref[...], own_ref[...], 1, 1).astype(BF16)
    out_ref[rows:] = dot(other_ref[...], own_ref[...], 1, 1).astype(BF16)


def rows_early_kernel(at_ref, cot_ref, other_ref, z1_ref, z2_ref, out_ref):
    me, rows = at_ref[0], cot_ref.shape[0]
    part = z1_ref.shape[1] // 2
    x, y = me & 1, me >> 1
    for t, tokens in enumerate((cot_ref, other_ref)):
        near_x, near_y = columns(tokens, x * part, part), columns(tokens, (2 + y) * part, part)
        for i, piece in enumerate((z1_ref, z2_ref)):
            total = dot(near_x, piece[:, :part], 1, 1) + dot(near_y, piece[:, part:], 1, 1)
            out_ref[pl.ds(t * rows, rows), pl.ds(i * HEAD, HEAD)] = total


def rows_late_kernel(
    at_ref, cot_ref, other_ref, own_ref, early_ref, z3_ref, x_ref, y_ref, keep_ref, low_ref, high_ref
):
    me, z, rows = at_ref[0], at_ref[2], cot_ref.shape[0]
    part = x_ref.shape[1]
    x, y = me & 1, me >> 1
    for t, tokens in ((1, other_ref), (0, cot_ref)):
        here = pl.ds(t * rows, rows)
        total = dot(columns(tokens, (1 - x) * part, part), x_ref[...], 1, 1)
        total = total + dot(columns(tokens, (3 - y) * part, part), y_ref[...], 1, 1)
        third = dot(columns(tokens, x * part, part), z3_ref[:, :part], 1, 1)
        third = third + dot(columns(tokens, (2 + y) * part, part), z3_ref[:, part:], 1, 1)
        heads = [
            own_ref[here, :],
            (total[:, :HEAD] + early_ref[here, :HEAD]).astype(BF16),
            (total[:, HEAD : 2 * HEAD] + early_ref[here, HEAD:]).astype(BF16),
            (total[:, 2 * HEAD :] + third).astype(BF16),
        ]
        for m, head in enumerate(heads):
            if t == 0:
                keep_ref[:, pl.ds(pl.multiple_of((z ^ m) * HEAD, HEAD), HEAD)] = head
            else:
                (low_ref, high_ref)[m // 2][:, m % 2 * HEAD : (m % 2 + 1) * HEAD] = head


def first_kernel(keep_a_ref, keep_b_ref, got_ref, a_ref, b_ref):
    for b, (keep, out) in enumerate(((keep_a_ref, a_ref), (keep_b_ref, b_ref))):
        out[...] = (keep[...] + got_ref[b].astype(F32)).astype(BF16)


def plane_kernel(keep_a_ref, keep_b_ref, got_ref, level_a_ref, level_b_ref, *outs):
    for b, (keep, level) in enumerate(((keep_a_ref, level_a_ref), (keep_b_ref, level_b_ref))):
        stay_ref, step_ref = outs[2 * b : 2 * b + 2]
        for m in range(4):
            total = keep[m] + got_ref[b, m].astype(F32) + level[m].astype(F32)
            if m % 2 == 0:
                stay_ref[m // 2] = total
            else:
                step_ref[m // 2] = total.astype(BF16)


def step_kernel(stay_ref, got_ref, total_ref, last_ref):
    total_ref[...] = stay_ref[0] + got_ref[0].astype(F32)
    last_ref[...] = (stay_ref[1] + got_ref[1].astype(F32)).astype(BF16)


def shard_kernel(a_ref, got_a_ref, b_ref, got_b_ref, out_ref):
    half = a_ref.shape[1]
    out_ref[:, :half] = (a_ref[...] + got_a_ref[...].astype(F32)).astype(BF16)
    out_ref[:, half:] = (b_ref[...] + got_b_ref[...].astype(F32)).astype(BF16)


def place_kernel(at_ref, *refs):
    *pieces, out_ref, wide_ref, sems = refs
    half = pieces[0].shape[1] // 2
    copies = []
    for s, piece in enumerate(pieces):
        peer = at_ref[0] ^ s
        x, y = peer & 1, peer >> 1
        for b, start in enumerate((2 * x + y, 4 + 2 * y + x)):
            place = pl.ds(pl.multiple_of(start * half, half), half)
            wide_ref[2 * s + b] = piece[:, b * half : (b + 1) * half].astype(F32)
            copies.append(pltpu.make_async_copy(wide_ref.at[2 * s + b], out_ref.at[:, place], sems.at[2 * s + b]))
            copies[-1].start()
    for copy in copies:
        copy.wait()


def swap(value, axis, mask):
    size = lax.axis_size(axis)
    return lax.ppermute(value, axis, [(i, i ^ mask) for i in range(size)])


def plane_body(queries, keys, values, cotangent, w_out, counts, dests):
    rows, width = queries.shape
    depth = cotangent.shape[1]
    part, half = depth // 4, depth // 8
    me, f = lax.axis_index("dp"), lax.axis_index("fsdp")
    at = jnp.stack([me, f, f >> 1, f & 1]).astype(jnp.int32)
    tokens = rows * lax.axis_size("dp") * lax.axis_size("fsdp")

    cot_other = swap(cotangent, "fsdp", 1)
    to_x, to_y = call(
        quarters_kernel,
        [shaped(rows, part)] * 2,
        [cotangent],
        name="quarters",
        mib=4,
        in_specs=[ANY],
        scratch_shapes=[pltpu.SemaphoreType.DMA((2,))],
    )
    cot_x, cot_y = swap(to_x, "dp", 1), swap(to_y, "dp", 2)
    probs = probs_of(counts, queries, keys, mib=12)
    out = call(
        outputs_kernel,
        shaped(rows + HEADER, width),
        [counts, dests, probs, values],
        name="outputs",
        mib=8,
        after=[cot_other],
    )
    out_x, out_y = swap(out, "dp", 1), swap(out, "dp", 2)

    mine = call(
        mine_kernel,
        shaped(HEAD, 2 * part),
        [w_out],
        name="mine",
        mib=4,
        weight=MINE_WEIGHT,
        after=[to_x],
        in_specs=[ANY],
        out_specs=VMEM,
        scratch_shapes=[pltpu.SemaphoreType.DMA((2,))],
    )
    z2, z1 = swap(mine, "fsdp", 4), swap(mine, "fsdp", 2)
    z3 = swap(z2, "fsdp", 2)
    own = call(
        rows_own_kernel,
        shaped(2 * rows, HEAD),
        [cotangent, cot_other, w_out],
        name="rows_own",
        mib=12,
        after=[out],
    )

    far_rows = call(
        far_kernel,
        shaped(LMAX, width),
        [at, counts, dests, out],
        name="far",
        mib=8,
        after=[cot_x, cot_y],
    )

    turn = turned(probs, mib=8, weight=TURN_WEIGHT, after=[own, far_rows, z1, z2])

    def term(r, after):
        return call(
            functools.partial(term_kernel, float(tokens) ** -0.5, r),
            [shaped(4, HEAD, half, dtype=F32)] * 2 + [shaped(2, 4, HEAD, half)],
            [at, cotangent, out, out_x, out_y, cot_x, cot_y],
            name="term%d" % r,
            mib=14,
            after=after,
        )

    *keeps, first = term(1, [turn])
    first = swap(first, "fsdp", 1)
    first_a, first_b = call(
        first_kernel,
        [shaped(4, HEAD, half)] * 2,
        [*keeps, first],
        name="first",
        mib=8,
    )
    *keeps, second = term(0, [keeps[0]])
    second = swap(second, "fsdp", 1)
    levels = swap(first_a, "dp", 2), swap(first_b, "dp", 1)

    early = call(
        rows_early_kernel,
        shaped(2 * rows, 2 * HEAD, dtype=F32),
        [at, cotangent, cot_other, z1, z2],
        name="rows_early",
        mib=12,
        after=[first_a],
    )
    three, three_token = call(
        attended_kernel,
        [shaped(4, LMAX, width), shaped(8, HEAD, dtype=F32)],
        [at, out, out_x, out_y],
        name="attended",
        mib=8,
        after=[first_a],
    )
    stay_a, step_a, stay_b, step_b = call(
        plane_kernel,
        [shaped(2, HEAD, half, dtype=F32), shaped(2, HEAD, half)] * 2,
        [*keeps, second, *levels],
        name="plane",
        mib=10,
        after=[early, three_token],
    )
    stays, steps = (stay_a, stay_b), (step_a, step_b)
    got = [swap(step, "fsdp", 2) for step in steps]

    to_x, to_y = call(
        pack_kernel,
        [shaped(3 * HEAD, part)] * 2,
        [z1, z2, z3],
        name="pack",
        mib=8,
        after=steps,
    )
    from_x, from_y = swap(to_x, "dp", 1), swap(to_y, "dp", 2)
    far = swap(far_rows, "dp", 3)

    totals = []
    for stay, step in zip(stays, got):
        total, last = call(
            step_kernel,
            [shaped(HEAD, half, dtype=F32), shaped(HEAD, half)],
            [stay, step],
            name="step",
            mib=4,
            weight=STEP_WEIGHT,
        )
        totals += [total, swap(last, "fsdp", 4)]

    attended, attended_token = call(
        across_kernel,
        [shaped(4, LMAX, width), shaped(8, HEAD, dtype=F32)],
        [three, far],
        name="across",
        mib=4,
        in_specs=[ANY, ANY],
        out_specs=[ANY, VMEM],
        scratch_shapes=[pltpu.SemaphoreType.DMA((1,))],
        input_output_aliases={0: 0},
    )
    shard = call(
        shard_kernel,
        shaped(HEAD, part),
        totals,
        name="shard",
        mib=4,
        after=[attended_token],
    )
    pieces = [shard] + [swap(shard, "dp", s) for s in (1, 2, 3)]
    grad_keep, *grad_send = call(
        rows_late_kernel,
        [shaped(rows, width // 2)] + [shaped(rows, width // 4)] * 2,
        [at, cotangent, cot_other, own, early, z3, from_x, from_y],
        name="rows_late",
        after=[shard],
        mib=12,
    )
    grad_other = [swap(part, "fsdp", 1) for part in grad_send]
    *grads, token = backward(at, probs, turn, queries, keys, values, grad_keep, *grad_other)
    weight_grad = call(
        place_kernel,
        shaped(HEAD, depth, dtype=F32),
        [at, *pieces],
        name="place",
        after=[token],
        mib=8,
        out_specs=ANY,
        scratch_shapes=[pltpu.VMEM((8, HEAD, half), F32), pltpu.SemaphoreType.DMA((8,))],
    )
    return (*grads, attended[None, None], weight_grad)


def body(queries, keys, values, cotangent, w_out, counts, dests):
    rows, width = queries.shape
    groups = counts.shape[1]
    tokens = rows * lax.axis_size("dp") * lax.axis_size("fsdp")
    probs = probs_of(counts, queries, keys, mib=48)
    out, slots = call(
        slots_kernel,
        [shaped(rows, width), shaped(groups, LMAX, width)],
        [counts, dests, probs, values],
        name="slots",
        mib=48,
    )
    attended = lax.all_to_all(slots, "dp", split_axis=0, concat_axis=0, tiled=True)
    product = dot(out, cotangent, 0, 0) * float(tokens) ** -0.5
    shard = lax.psum_scatter(product.astype(BF16), "fsdp", scatter_dimension=0, tiled=True)
    weight_grad = lax.psum(shard, "dp").astype(F32)
    grad_rows = dot(cotangent, lax.all_gather(w_out, "fsdp", axis=0, tiled=True), 1, 1).astype(BF16)
    *grads, token = backward(None, probs, turned(probs, mib=48), queries, keys, values, grad_rows, mib=48)
    return (*grads, attended[None, None], weight_grad)


def solution(mesh):
    placed = (
        P(("dp", "fsdp"), None),
        P(("dp", "fsdp"), None),
        P(("dp", "fsdp"), None),
        P(("dp", "fsdp"), None),
        P("fsdp", None),
        P(("dp", "fsdp"), None),
        P(("dp", "fsdp"), None),
    )
    plane = mesh.shape["dp"] == 4 and mesh.shape["fsdp"] == HEADS
    return jax.shard_map(
        plane_body if plane else body,
        mesh=mesh,
        in_specs=placed,
        out_specs=(
            P(("dp", "fsdp"), None),
            P(("dp", "fsdp"), None),
            P(("dp", "fsdp"), None),
            P("dp", "fsdp", None, None, None),
            P("fsdp", None),
        ),
        check_vma=False,
    )
```

```python
import functools

import jax
import jax.numpy as jnp
from jax import lax
from jax.experimental import pallas as pl
from jax.experimental.pallas import tpu as pltpu
from jax.sharding import PartitionSpec as P

HEADS = 8
LMAX = 128
HEAD = 128
HEADER = 16
MIB = 1024 * 1024
MINE_WEIGHT = 12 * 10**9
TURN_WEIGHT = 23 * 10**9
ATTENDED_WEIGHT = 23 * 10**9
PLANE_WEIGHT = 23000000000
EARLY_WEIGHT = 0
TERM_WEIGHT = 0
STEP_WEIGHT = 23 * 10**9

F32 = jnp.float32
BF16 = jnp.bfloat16
SMEM = pl.BlockSpec(memory_space=pltpu.SMEM)
VMEM = pl.BlockSpec(memory_space=pltpu.VMEM)
ANY = pl.BlockSpec(memory_space=pl.ANY)


def dot(a, b, ca, cb):
    return lax.dot_general(a, b, (((ca,), (cb,)), ((), ())), preferred_element_type=F32)


def call(kernel, out_shape, args, name, mib=24, after=(), weight=0, **more):
    single = not isinstance(out_shape, (list, tuple))
    given = len(args)
    more.setdefault("in_specs", [SMEM if a.dtype == jnp.int32 else VMEM for a in args])
    more.setdefault("out_specs", VMEM if single else [VMEM] * len(out_shape))
    more["in_specs"] = more["in_specs"] + [ANY] * len(after)

    def run(*refs):
        kernel(*refs[:given], *refs[given + len(after) :])

    return pl.pallas_call(
        run,
        out_shape=out_shape,
        compiler_params=pltpu.CompilerParams(vmem_limit_bytes=mib * MIB),
        cost_estimate=pl.CostEstimate(flops=weight, bytes_accessed=1, transcendentals=0),
        name=name,
        **more,
    )(*args, *after)


def shaped(*shape, dtype=BF16):
    return jax.ShapeDtypeStruct(shape, dtype)


def ahead(count, make, use):
    made = make(0)
    for i in range(count):
        following = make(i + 1) if i + 1 < count else None
        use(i, made)
        made = following


def image_of(index, counts_ref):
    image = jnp.zeros_like(index)
    end = 0
    for g in range(counts_ref.shape[1]):
        end = end + counts_ref[0, g]
        image = image + (index >= end).astype(jnp.int32)
    return image


def image_rows(start, count, out):
    rows = out.shape[0]
    place = lax.broadcasted_iota(jnp.int32, (LMAX, rows), 0)
    index = lax.broadcasted_iota(jnp.int32, (LMAX, rows), 1)
    chosen = (index == place + start) & (place < count)
    return dot(jnp.where(chosen, 1.0, 0.0).astype(BF16), out, 1, 0).astype(BF16)


def probs_kernel(counts_ref, q_ref, k_ref, probs_ref):
    rows = q_ref.shape[0]
    scale = float(HEAD) ** -0.5
    image_r = image_of(lax.broadcasted_iota(jnp.int32, (rows, 1), 0), counts_ref)
    image_c = image_of(lax.broadcasted_iota(jnp.int32, (1, rows), 1), counts_ref)
    same = image_r == image_c

    def make(h):
        cols = pl.ds(h * HEAD, HEAD)
        return dot(q_ref[:, cols], k_ref[:, cols], 1, 1)

    def use(h, scores):
        scores = jnp.where(same, scores * scale, -1e30)
        top = jnp.max(scores, axis=1, keepdims=True)
        weights = jnp.exp(scores - top)
        probs_ref[h] = weights * (1.0 / jnp.sum(weights, axis=1, keepdims=True))

    ahead(HEADS, make, use)


def outputs_of(probs_ref, v_ref, out_ref):
    rows = v_ref.shape[0]

    def make(h):
        return dot(probs_ref[h].astype(BF16), v_ref[:, pl.ds(h * HEAD, HEAD)], 1, 0)

    def use(h, value):
        out_ref[:rows, pl.ds(h * HEAD, HEAD)] = value.astype(BF16)

    ahead(HEADS, make, use)


def quarters_kernel(cot_ref, x_ref, y_ref, sems):
    part = x_ref.shape[1]
    me = lax.axis_index("dp")
    starts = (1 - (me & 1)) * part, (3 - (me >> 1)) * part
    pairs = [
        (cot_ref.at[:, pl.ds(pl.multiple_of(start, HEAD), part)], out)
        for start, out in zip(starts, (x_ref, y_ref))
    ]
    copy_all(pairs, sems)


def outputs_kernel(counts_ref, dests_ref, probs_ref, v_ref, out_ref):
    outputs_of(probs_ref, v_ref, out_ref)
    rows, width = v_ref.shape
    index = lax.broadcasted_iota(jnp.int32, (HEADER, width), 1)
    line = lax.broadcasted_iota(jnp.int32, (HEADER, width), 0)
    place, group = index, jnp.full((HEADER, width), dests_ref[0, 0], jnp.int32)
    start = 0
    for g in range(counts_ref.shape[1]):
        count, dest = counts_ref[0, g], dests_ref[0, g]
        past = index >= start
        group = jnp.where(past, dest, group)
        place = jnp.where(past, index - start, place)
        start = start + count
    header = jnp.where(line == 0, place, jnp.where(line == 1, group, 0))
    out_ref[rows:, :] = jnp.where(index < rows, header, -1).astype(F32).astype(BF16)


def far_kernel(at_ref, counts_ref, dests_ref, out_ref, far_ref):
    start, far_start, far_count = 0, 0, 0
    for g in range(counts_ref.shape[1]):
        count = counts_ref[0, g]
        far = dests_ref[0, g] == (at_ref[0] ^ 3)
        far_start = jnp.where(far, start, far_start)
        far_count = jnp.where(far, count, far_count)
        start = start + count
    far_ref[...] = image_rows(far_start, far_count, out_ref[: out_ref.shape[0] - HEADER])


def slots_kernel(counts_ref, dests_ref, probs_ref, v_ref, out_ref, slots_ref):
    outputs_of(probs_ref, v_ref, out_ref)
    start = 0
    for g in range(counts_ref.shape[1]):
        count = counts_ref[0, g]
        slots_ref[dests_ref[0, g]] = image_rows(start, count, out_ref[...])
        start = start + count


def probs_of(counts, queries, keys, **more):
    rows, width = queries.shape
    return call(
        probs_kernel,
        shaped(HEADS, rows, rows, dtype=F32),
        [counts, queries, keys],
        name="probs",
        **more,
    )


def turn_kernel(probs_ref, out_ref):
    for h in range(HEADS):
        out_ref[h] = probs_ref[h].T.astype(BF16)


def turned(probs, **more):
    heads, rows, _ = probs.shape
    return call(turn_kernel, shaped(heads, rows, rows), [probs], name="turn", **more)


def backward_kernel(split, *refs):
    if split:
        at_ref, *refs = refs
    probs_ref, turned_ref, q_ref, k_ref, v_ref, *grads = refs[:-8]
    token_ref, *kept, sems = refs[-5:]
    outs = refs[-8:-5]
    token_ref[...] = jnp.zeros_like(token_ref)
    scale = float(HEAD) ** -0.5
    copies = []

    def make(h):
        if split:
            own = grads[0][:, h // 2 * HEAD : (h // 2 + 1) * HEAD]
            near = (h // 2) ^ at_ref[2]
            near_cols = pl.ds(pl.multiple_of((near & 1) * HEAD, HEAD), HEAD)
            other = jnp.where(near < 2, grads[1][:, near_cols], grads[2][:, near_cols])
            grad = jnp.where(at_ref[3] == h % 2, own, other)
        else:
            grad = grads[0][:, h * HEAD : (h + 1) * HEAD]
        return grad, dot(grad, v_ref[:, pl.ds(h * HEAD, HEAD)], 1, 1)

    def use(h, made):
        grad, dprobs = made
        cols = pl.ds(h * HEAD, HEAD)
        probs = probs_ref[h]
        delta = jnp.sum(probs * dprobs, axis=1, keepdims=True)
        dscores = (probs * (dprobs - delta) * scale).astype(BF16)
        values = (
            dot(dscores, k_ref[:, cols], 1, 0),
            dot(dscores, q_ref[:, cols], 0, 0),
            dot(turned_ref[h], grad, 1, 0),
        )
        for i, (value, keep, out) in enumerate(zip(values, kept, outs)):
            keep[:, cols] = value.astype(BF16)
            if h % 2 == 1:
                pair = pl.ds((h - 1) * HEAD, 2 * HEAD)
                copies.append(pltpu.make_async_copy(keep.at[:, pair], out.at[:, pair], sems.at[i, h // 2]))
                copies[-1].start()

    ahead(HEADS, make, use)
    for copy in copies:
        copy.wait()


def backward(at, probs, turn, queries, keys, values, *grads, mib=14):
    rows, width = queries.shape
    split = at is not None
    return call(
        functools.partial(backward_kernel, split),
        [shaped(rows, width)] * 3 + [shaped(8, HEAD, dtype=F32)],
        ([at] if split else []) + [probs, turn, queries, keys, values, *grads],
        name="backward",
        mib=mib,
        out_specs=[ANY] * 3 + [VMEM],
        scratch_shapes=[pltpu.VMEM((rows, width), BF16)] * 3 + [pltpu.SemaphoreType.DMA((3, HEADS // 2))],
    )


def attended_kernel(at_ref, own_ref, x_ref, y_ref, out_ref, token_ref):
    token_ref[...] = jnp.zeros_like(token_ref)
    rows = own_ref.shape[0] - HEADER
    me = at_ref[0]
    place = lax.broadcasted_iota(jnp.int32, (LMAX, rows), 0)
    sources = own_ref, x_ref, y_ref

    def make(s):
        header = sources[s][rows:, :rows].astype(F32).astype(jnp.int32)
        chosen = (header[0:1] == place) & (header[1:2] == me)
        return dot(jnp.where(chosen, 1.0, 0.0).astype(BF16), sources[s][:rows, :], 1, 0)

    def use(s, value):
        out_ref[me ^ s] = value.astype(BF16)

    ahead(3, make, use)


def across_kernel(three_ref, far_ref, out_ref, token_ref, sems):
    token_ref[...] = jnp.zeros_like(token_ref)
    copy_all([(far_ref, out_ref.at[lax.axis_index("dp") ^ 3])], sems)


def columns(ref, start, size):
    return ref[:, pl.ds(pl.multiple_of(start, HEAD), size)]


def copy_all(pairs, sems):
    copies = [pltpu.make_async_copy(a, b, sems.at[i]) for i, (a, b) in enumerate(pairs)]
    for copy in copies:
        copy.start()
    for copy in copies:
        copy.wait()


def mine_kernel(w_ref, out_ref, sems):
    part = out_ref.shape[1] // 2
    me = lax.axis_index("dp")
    starts = (me & 1) * part, (2 + (me >> 1)) * part
    pairs = [
        (w_ref.at[:, pl.ds(pl.multiple_of(start, HEAD), part)], out_ref.at[:, pl.ds(i * part, part)])
        for i, start in enumerate(starts)
    ]
    copy_all(pairs, sems)


def pack_kernel(z1_ref, z2_ref, z3_ref, x_ref, y_ref):
    part = x_ref.shape[1]
    for m, piece in enumerate((z1_ref, z2_ref, z3_ref)):
        x_ref[pl.ds(m * HEAD, HEAD)] = piece[:, :part]
        y_ref[pl.ds(m * HEAD, HEAD)] = piece[:, part:]


def term_kernel(b, r, at_ref, cot_ref, own_ref, near_ref, near_cot_ref, keep_ref, send_ref):
    rows, part = near_cot_ref.shape
    half = part // 2
    x, y, z, c = at_ref[0] & 1, at_ref[0] >> 1, at_ref[2], at_ref[3]
    place, inner = (x, y ^ r) if b == 0 else (2 + y, x ^ r)
    own_cot = columns(cot_ref, place * part + inner * half, half)
    near_cot = columns(near_cot_ref, inner * half, half)
    outs = send_ref, keep_ref

    def make(i):
        head = ((z ^ (i // 2)) * 2 + (c ^ (1 - i % 2))) * HEAD
        total = dot(columns(own_ref, head, HEAD)[:rows], own_cot, 0, 0)
        return total + dot(columns(near_ref, head, HEAD)[:rows], near_cot, 0, 0)

    def use(i, total):
        outs[i % 2][i // 2] = total.astype(outs[i % 2].dtype)

    ahead(8, make, use)


def rows_own_kernel(cot_ref, other_ref, own_ref, out_ref):
    rows = cot_ref.shape[0]
    out_ref[:rows] = dot(cot_ref[...], own_ref[...], 1, 1).astype(BF16)
    out_ref[rows:] = dot(other_ref[...], own_ref[...], 1, 1).astype(BF16)


def rows_early_kernel(at_ref, cot_ref, other_ref, z1_ref, z2_ref, out_ref):
    me, rows = at_ref[0], cot_ref.shape[0]
    part = z1_ref.shape[1] // 2
    x, y = me & 1, me >> 1
    pieces, tokens = (z1_ref, z2_ref), (cot_ref, other_ref)

    def make(i):
        piece, token = pieces[i % 2], tokens[i // 2]
        total = dot(columns(token, x * part, part), piece[:, :part], 1, 1)
        return total + dot(columns(token, (2 + y) * part, part), piece[:, part:], 1, 1)

    def use(i, total):
        out_ref[pl.ds(i // 2 * rows, rows), pl.ds(i % 2 * HEAD, HEAD)] = total

    ahead(4, make, use)


def rows_late_kernel(
    at_ref, cot_ref, other_ref, own_ref, early_ref, z3_ref, x_ref, y_ref, keep_ref, low_ref, high_ref
):
    me, z, rows = at_ref[0], at_ref[2], cot_ref.shape[0]
    part = x_ref.shape[1]
    x, y = me & 1, me >> 1
    order = (1, other_ref), (0, cot_ref)

    def make(i):
        token = order[i][1]
        total = dot(columns(token, (1 - x) * part, part), x_ref[...], 1, 1)
        total = total + dot(columns(token, (3 - y) * part, part), y_ref[...], 1, 1)
        third = dot(columns(token, x * part, part), z3_ref[:, :part], 1, 1)
        return total, third + dot(columns(token, (2 + y) * part, part), z3_ref[:, part:], 1, 1)

    def use(i, made):
        t, (total, third) = order[i][0], made
        here = pl.ds(t * rows, rows)
        heads = [
            own_ref[here, :],
            (total[:, :HEAD] + early_ref[here, :HEAD]).astype(BF16),
            (total[:, HEAD : 2 * HEAD] + early_ref[here, HEAD:]).astype(BF16),
            (total[:, 2 * HEAD :] + third).astype(BF16),
        ]
        for m, head in enumerate(heads):
            if t == 0:
                keep_ref[:, pl.ds(pl.multiple_of((z ^ m) * HEAD, HEAD), HEAD)] = head
            else:
                (low_ref, high_ref)[m // 2][:, m % 2 * HEAD : (m % 2 + 1) * HEAD] = head

    ahead(2, make, use)


def first_kernel(keep_ref, got_ref, out_ref):
    out_ref[...] = (keep_ref[...] + got_ref[...].astype(F32)).astype(BF16)


def plane_kernel(keep_ref, got_ref, level_ref, stay_ref, step_ref):
    for m in range(4):
        total = keep_ref[m] + got_ref[m].astype(F32) + level_ref[m].astype(F32)
        if m % 2 == 0:
            stay_ref[m // 2] = total
        else:
            step_ref[m // 2] = total.astype(BF16)


def step_kernel(stay_ref, got_ref, total_ref, last_ref):
    total_ref[...] = stay_ref[0] + got_ref[0].astype(F32)
    last_ref[...] = (stay_ref[1] + got_ref[1].astype(F32)).astype(BF16)


def shard_kernel(scale, a_ref, got_a_ref, b_ref, got_b_ref, out_ref):
    half = a_ref.shape[1]
    out_ref[:, :half] = ((a_ref[...] + got_a_ref[...].astype(F32)) * scale).astype(BF16)
    out_ref[:, half:] = ((b_ref[...] + got_b_ref[...].astype(F32)) * scale).astype(BF16)


def place_kernel(at_ref, *refs):
    *pieces, out_ref, wide_ref, sems = refs
    half = pieces[0].shape[1] // 2
    copies = []
    for s, piece in enumerate(pieces):
        peer = at_ref[0] ^ s
        x, y = peer & 1, peer >> 1
        for b, start in enumerate((2 * x + y, 4 + 2 * y + x)):
            place = pl.ds(pl.multiple_of(start * half, half), half)
            wide_ref[2 * s + b] = piece[:, b * half : (b + 1) * half].astype(F32)
            copies.append(pltpu.make_async_copy(wide_ref.at[2 * s + b], out_ref.at[:, place], sems.at[2 * s + b]))
            copies[-1].start()
    for copy in copies:
        copy.wait()


def swap(value, axis, mask):
    size = lax.axis_size(axis)
    return lax.ppermute(value, axis, [(i, i ^ mask) for i in range(size)])


def plane_body(queries, keys, values, cotangent, w_out, counts, dests):
    rows, width = queries.shape
    depth = cotangent.shape[1]
    part, half = depth // 4, depth // 8
    me, f = lax.axis_index("dp"), lax.axis_index("fsdp")
    at = jnp.stack([me, f, f >> 1, f & 1]).astype(jnp.int32)
    tokens = rows * lax.axis_size("dp") * lax.axis_size("fsdp")

    cot_other = swap(cotangent, "fsdp", 1)
    to_x, to_y = call(
        quarters_kernel,
        [shaped(rows, part)] * 2,
        [cotangent],
        name="quarters",
        mib=4,
        in_specs=[ANY],
        scratch_shapes=[pltpu.SemaphoreType.DMA((2,))],
    )
    cot_x, cot_y = swap(to_x, "dp", 1), swap(to_y, "dp", 2)
    probs = probs_of(counts, queries, keys, mib=12)
    out = call(
        outputs_kernel,
        shaped(rows + HEADER, width),
        [counts, dests, probs, values],
        name="outputs",
        mib=8,
        after=[cot_other],
    )
    out_x, out_y = swap(out, "dp", 1), swap(out, "dp", 2)

    mine = call(
        mine_kernel,
        shaped(HEAD, 2 * part),
        [w_out],
        name="mine",
        mib=4,
        weight=MINE_WEIGHT,
        after=[to_x],
        in_specs=[ANY],
        out_specs=VMEM,
        scratch_shapes=[pltpu.SemaphoreType.DMA((2,))],
    )
    z2, z1 = swap(mine, "fsdp", 4), swap(mine, "fsdp", 2)
    z3 = swap(z2, "fsdp", 2)
    own = call(
        rows_own_kernel,
        shaped(2 * rows, HEAD),
        [cotangent, cot_other, w_out],
        name="rows_own",
        mib=12,
        after=[out],
    )

    far_rows = call(
        far_kernel,
        shaped(LMAX, width),
        [at, counts, dests, out],
        name="far",
        mib=8,
        after=[cot_x, cot_y],
    )

    turn = turned(probs, mib=8, weight=TURN_WEIGHT, after=[own, far_rows, z2])

    def term(b, r, after):
        return call(
            functools.partial(term_kernel, b, r),
            [shaped(4, HEAD, half, dtype=F32), shaped(4, HEAD, half)],
            [at, cotangent, out, (out_x, out_y)[b], (cot_x, cot_y)[b]],
            name="term%d%d" % (b, r),
            mib=12,
            weight=TERM_WEIGHT if (b, r) == (1, 0) else 0,
            after=after,
        )

    firsts, order = [], [turn]
    for b in range(2):
        keep, send = term(b, 1, order)
        order = [keep, z1]
        firsts.append((keep, swap(send, "fsdp", 1)))
    going = [
        call(first_kernel, shaped(4, HEAD, half), list(pair), name="first", mib=8) for pair in firsts
    ]
    levels = swap(going[0], "dp", 2), swap(going[1], "dp", 1)
    seconds = []
    for b in range(2):
        keep, send = term(b, 0, order + [going[b]])
        order = [keep]
        seconds.append((keep, swap(send, "fsdp", 1)))

    early = call(
        rows_early_kernel,
        shaped(2 * rows, 2 * HEAD, dtype=F32),
        [at, cotangent, cot_other, z1, z2],
        name="rows_early",
        mib=12,
        weight=EARLY_WEIGHT,
        after=going,
    )
    three, three_token = call(
        attended_kernel,
        [shaped(4, LMAX, width), shaped(8, HEAD, dtype=F32)],
        [at, out, out_x, out_y],
        name="attended",
        mib=8,
        weight=ATTENDED_WEIGHT,
        after=going,
    )
    stays, steps, order = [], [], [early, three_token]
    for (keep, second), level in zip(seconds, levels):
        stay, step = call(
            plane_kernel,
            [shaped(2, HEAD, half, dtype=F32), shaped(2, HEAD, half)],
            [keep, second, level],
            name="plane%d" % len(steps),
            mib=8,
            weight=PLANE_WEIGHT if steps else 0,
            after=order,
        )
        stays.append(stay)
        steps.append(step)
        order = [stay]
    got = [swap(step, "fsdp", 2) for step in steps]

    to_x, to_y = call(
        pack_kernel,
        [shaped(3 * HEAD, part)] * 2,
        [z1, z2, z3],
        name="pack",
        mib=8,
        after=steps,
    )
    from_x, from_y = swap(to_x, "dp", 1), swap(to_y, "dp", 2)
    far = swap(far_rows, "dp", 3)

    totals, lasts = [], []
    for stay, step in zip(stays, got):
        total, last = call(
            step_kernel,
            [shaped(HEAD, half, dtype=F32), shaped(HEAD, half)],
            [stay, step],
            name="step",
            mib=4,
            weight=0 if totals else STEP_WEIGHT,
            after=[] if totals else [far],
        )
        totals += [total, swap(last, "fsdp", 4)]
        lasts.append(last)

    attended, attended_token = call(
        across_kernel,
        [shaped(4, LMAX, width), shaped(8, HEAD, dtype=F32)],
        [three, far],
        name="across",
        mib=4,
        after=lasts,
        in_specs=[ANY, ANY],
        out_specs=[ANY, VMEM],
        scratch_shapes=[pltpu.SemaphoreType.DMA((1,))],
        input_output_aliases={0: 0},
    )
    shard = call(
        functools.partial(shard_kernel, float(tokens) ** -0.5),
        shaped(HEAD, part),
        totals,
        name="shard",
        mib=4,
        after=[attended_token],
    )
    pieces = [shard] + [swap(shard, "dp", s) for s in (1, 2, 3)]
    grad_keep, *grad_send = call(
        rows_late_kernel,
        [shaped(rows, width // 2)] + [shaped(rows, width // 4)] * 2,
        [at, cotangent, cot_other, own, early, z3, from_x, from_y],
        name="rows_late",
        after=[shard],
        mib=12,
    )
    grad_other = [swap(part, "fsdp", 1) for part in grad_send]
    *grads, token = backward(at, probs, turn, queries, keys, values, grad_keep, *grad_other)
    weight_grad = call(
        place_kernel,
        shaped(HEAD, depth, dtype=F32),
        [at, *pieces],
        name="place",
        after=[token],
        mib=8,
        out_specs=ANY,
        scratch_shapes=[pltpu.VMEM((8, HEAD, half), F32), pltpu.SemaphoreType.DMA((8,))],
    )
    return (*grads, attended[None, None], weight_grad)


def body(queries, keys, values, cotangent, w_out, counts, dests):
    rows, width = queries.shape
    groups = counts.shape[1]
    tokens = rows * lax.axis_size("dp") * lax.axis_size("fsdp")
    probs = probs_of(counts, queries, keys, mib=48)
    out, slots = call(
        slots_kernel,
        [shaped(rows, width), shaped(groups, LMAX, width)],
        [counts, dests, probs, values],
        name="slots",
        mib=48,
    )
    attended = lax.all_to_all(slots, "dp", split_axis=0, concat_axis=0, tiled=True)
    product = dot(out, cotangent, 0, 0) * float(tokens) ** -0.5
    shard = lax.psum_scatter(product.astype(BF16), "fsdp", scatter_dimension=0, tiled=True)
    weight_grad = lax.psum(shard, "dp").astype(F32)
    grad_rows = dot(cotangent, lax.all_gather(w_out, "fsdp", axis=0, tiled=True), 1, 1).astype(BF16)
    *grads, token = backward(None, probs, turned(probs, mib=48), queries, keys, values, grad_rows, mib=48)
    return (*grads, attended[None, None], weight_grad)


def solution(mesh):
    placed = (
        P(("dp", "fsdp"), None),
        P(("dp", "fsdp"), None),
        P(("dp", "fsdp"), None),
        P(("dp", "fsdp"), None),
        P("fsdp", None),
        P(("dp", "fsdp"), None),
        P(("dp", "fsdp"), None),
    )
    plane = mesh.shape["dp"] == 4 and mesh.shape["fsdp"] == HEADS
    return jax.shard_map(
        plane_body if plane else body,
        mesh=mesh,
        in_specs=placed,
        out_specs=(
            P(("dp", "fsdp"), None),
            P(("dp", "fsdp"), None),
            P(("dp", "fsdp"), None),
            P("dp", "fsdp", None, None, None),
            P("fsdp", None),
        ),
        check_vma=False,
    )
```

```python
import functools

import jax
import jax.numpy as jnp
from jax import lax
from jax.experimental import pallas as pl
from jax.experimental.pallas import tpu as pltpu
from jax.sharding import PartitionSpec as P

HEADS = 8
LMAX = 128
HEAD = 128
HEADER = 16
MIB = 1024 * 1024
MINE_WEIGHT = 12 * 10**9
TURN_WEIGHT = 23 * 10**9
ATTENDED_WEIGHT = 0
PLANE_WEIGHT = 23000000000
EARLY_WEIGHT = 23000000000
TERM_WEIGHT = 0
STEP_WEIGHT = 23 * 10**9

F32 = jnp.float32
BF16 = jnp.bfloat16
SMEM = pl.BlockSpec(memory_space=pltpu.SMEM)
VMEM = pl.BlockSpec(memory_space=pltpu.VMEM)
ANY = pl.BlockSpec(memory_space=pl.ANY)


def dot(a, b, ca, cb):
    return lax.dot_general(a, b, (((ca,), (cb,)), ((), ())), preferred_element_type=F32)


def call(kernel, out_shape, args, name, mib=24, after=(), weight=0, **more):
    single = not isinstance(out_shape, (list, tuple))
    given = len(args)
    more.setdefault("in_specs", [SMEM if a.dtype == jnp.int32 else VMEM for a in args])
    more.setdefault("out_specs", VMEM if single else [VMEM] * len(out_shape))
    more["in_specs"] = more["in_specs"] + [ANY] * len(after)

    def run(*refs):
        kernel(*refs[:given], *refs[given + len(after) :])

    return pl.pallas_call(
        run,
        out_shape=out_shape,
        compiler_params=pltpu.CompilerParams(vmem_limit_bytes=mib * MIB),
        cost_estimate=pl.CostEstimate(flops=weight, bytes_accessed=1, transcendentals=0),
        name=name,
        **more,
    )(*args, *after)


def shaped(*shape, dtype=BF16):
    return jax.ShapeDtypeStruct(shape, dtype)


def ahead(count, make, use):
    made = make(0)
    for i in range(count):
        following = make(i + 1) if i + 1 < count else None
        use(i, made)
        made = following


def image_of(index, counts_ref):
    image = jnp.zeros_like(index)
    end = 0
    for g in range(counts_ref.shape[1]):
        end = end + counts_ref[0, g]
        image = image + (index >= end).astype(jnp.int32)
    return image


def image_rows(start, count, out):
    rows = out.shape[0]
    place = lax.broadcasted_iota(jnp.int32, (LMAX, rows), 0)
    index = lax.broadcasted_iota(jnp.int32, (LMAX, rows), 1)
    chosen = (index == place + start) & (place < count)
    return dot(jnp.where(chosen, 1.0, 0.0).astype(BF16), out, 1, 0).astype(BF16)


def probs_kernel(counts_ref, q_ref, k_ref, probs_ref):
    rows = q_ref.shape[0]
    scale = float(HEAD) ** -0.5
    image_r = image_of(lax.broadcasted_iota(jnp.int32, (rows, 1), 0), counts_ref)
    image_c = image_of(lax.broadcasted_iota(jnp.int32, (1, rows), 1), counts_ref)
    same = image_r == image_c

    def make(h):
        cols = pl.ds(h * HEAD, HEAD)
        return dot(q_ref[:, cols], k_ref[:, cols], 1, 1)

    def use(h, scores):
        scores = jnp.where(same, scores * scale, -1e30)
        top = jnp.max(scores, axis=1, keepdims=True)
        weights = jnp.exp(scores - top)
        probs_ref[h] = weights * (1.0 / jnp.sum(weights, axis=1, keepdims=True))

    ahead(HEADS, make, use)


def outputs_of(probs_ref, v_ref, out_ref):
    rows = v_ref.shape[0]

    def make(h):
        return dot(probs_ref[h].astype(BF16), v_ref[:, pl.ds(h * HEAD, HEAD)], 1, 0)

    def use(h, value):
        out_ref[:rows, pl.ds(h * HEAD, HEAD)] = value.astype(BF16)

    ahead(HEADS, make, use)


def quarters_kernel(cot_ref, x_ref, y_ref, sems):
    part = x_ref.shape[1]
    me = lax.axis_index("dp")
    starts = (1 - (me & 1)) * part, (3 - (me >> 1)) * part
    pairs = [
        (cot_ref.at[:, pl.ds(pl.multiple_of(start, HEAD), part)], out)
        for start, out in zip(starts, (x_ref, y_ref))
    ]
    copy_all(pairs, sems)


def outputs_kernel(counts_ref, dests_ref, probs_ref, v_ref, out_ref):
    outputs_of(probs_ref, v_ref, out_ref)
    rows, width = v_ref.shape
    index = lax.broadcasted_iota(jnp.int32, (HEADER, width), 1)
    line = lax.broadcasted_iota(jnp.int32, (HEADER, width), 0)
    place, group = index, jnp.full((HEADER, width), dests_ref[0, 0], jnp.int32)
    start = 0
    for g in range(counts_ref.shape[1]):
        count, dest = counts_ref[0, g], dests_ref[0, g]
        past = index >= start
        group = jnp.where(past, dest, group)
        place = jnp.where(past, index - start, place)
        start = start + count
    header = jnp.where(line == 0, place, jnp.where(line == 1, group, 0))
    out_ref[rows:, :] = jnp.where(index < rows, header, -1).astype(F32).astype(BF16)


def far_kernel(at_ref, counts_ref, dests_ref, out_ref, far_ref):
    start, far_start, far_count = 0, 0, 0
    for g in range(counts_ref.shape[1]):
        count = counts_ref[0, g]
        far = dests_ref[0, g] == (at_ref[0] ^ 3)
        far_start = jnp.where(far, start, far_start)
        far_count = jnp.where(far, count, far_count)
        start = start + count
    far_ref[...] = image_rows(far_start, far_count, out_ref[: out_ref.shape[0] - HEADER])


def slots_kernel(counts_ref, dests_ref, probs_ref, v_ref, out_ref, slots_ref):
    outputs_of(probs_ref, v_ref, out_ref)
    start = 0
    for g in range(counts_ref.shape[1]):
        count = counts_ref[0, g]
        slots_ref[dests_ref[0, g]] = image_rows(start, count, out_ref[...])
        start = start + count


def probs_of(counts, queries, keys, **more):
    rows, width = queries.shape
    return call(
        probs_kernel,
        shaped(HEADS, rows, rows, dtype=F32),
        [counts, queries, keys],
        name="probs",
        **more,
    )


def turn_kernel(probs_ref, out_ref):
    for h in range(HEADS):
        out_ref[h] = probs_ref[h].T.astype(BF16)


def turned(probs, **more):
    heads, rows, _ = probs.shape
    return call(turn_kernel, shaped(heads, rows, rows), [probs], name="turn", **more)


def backward_kernel(split, *refs):
    if split:
        at_ref, *refs = refs
    probs_ref, turned_ref, q_ref, k_ref, v_ref, *grads = refs[:-8]
    token_ref, *kept, sems = refs[-5:]
    outs = refs[-8:-5]
    token_ref[...] = jnp.zeros_like(token_ref)
    scale = float(HEAD) ** -0.5
    copies = []

    def make(h):
        if split:
            own = grads[0][:, h // 2 * HEAD : (h // 2 + 1) * HEAD]
            near = (h // 2) ^ at_ref[2]
            near_cols = pl.ds(pl.multiple_of((near & 1) * HEAD, HEAD), HEAD)
            other = jnp.where(near < 2, grads[1][:, near_cols], grads[2][:, near_cols])
            grad = jnp.where(at_ref[3] == h % 2, own, other)
        else:
            grad = grads[0][:, h * HEAD : (h + 1) * HEAD]
        return grad, dot(grad, v_ref[:, pl.ds(h * HEAD, HEAD)], 1, 1)

    def use(h, made):
        grad, dprobs = made
        cols = pl.ds(h * HEAD, HEAD)
        probs = probs_ref[h]
        delta = jnp.sum(probs * dprobs, axis=1, keepdims=True)
        dscores = (probs * (dprobs - delta) * scale).astype(BF16)
        values = (
            dot(dscores, k_ref[:, cols], 1, 0),
            dot(dscores, q_ref[:, cols], 0, 0),
            dot(turned_ref[h], grad, 1, 0),
        )
        for i, (value, keep, out) in enumerate(zip(values, kept, outs)):
            keep[:, cols] = value.astype(BF16)
            if h % 2 == 1:
                pair = pl.ds((h - 1) * HEAD, 2 * HEAD)
                copies.append(pltpu.make_async_copy(keep.at[:, pair], out.at[:, pair], sems.at[i, h // 2]))
                copies[-1].start()

    ahead(HEADS, make, use)
    for copy in copies:
        copy.wait()


def backward(at, probs, turn, queries, keys, values, *grads, mib=14):
    rows, width = queries.shape
    split = at is not None
    return call(
        functools.partial(backward_kernel, split),
        [shaped(rows, width)] * 3 + [shaped(8, HEAD, dtype=F32)],
        ([at] if split else []) + [probs, turn, queries, keys, values, *grads],
        name="backward",
        mib=mib,
        out_specs=[ANY] * 3 + [VMEM],
        scratch_shapes=[pltpu.VMEM((rows, width), BF16)] * 3 + [pltpu.SemaphoreType.DMA((3, HEADS // 2))],
    )


def attended_kernel(at_ref, own_ref, x_ref, y_ref, out_ref, token_ref):
    token_ref[...] = jnp.zeros_like(token_ref)
    rows = own_ref.shape[0] - HEADER
    me = at_ref[0]
    place = lax.broadcasted_iota(jnp.int32, (LMAX, rows), 0)
    sources = own_ref, x_ref, y_ref

    def make(s):
        header = sources[s][rows:, :rows].astype(F32).astype(jnp.int32)
        chosen = (header[0:1] == place) & (header[1:2] == me)
        return dot(jnp.where(chosen, 1.0, 0.0).astype(BF16), sources[s][:rows, :], 1, 0)

    def use(s, value):
        out_ref[me ^ s] = value.astype(BF16)

    ahead(3, make, use)


def across_kernel(three_ref, far_ref, out_ref, token_ref, sems):
    token_ref[...] = jnp.zeros_like(token_ref)
    copy_all([(far_ref, out_ref.at[lax.axis_index("dp") ^ 3])], sems)


def columns(ref, start, size):
    return ref[:, pl.ds(pl.multiple_of(start, HEAD), size)]


def copy_all(pairs, sems):
    copies = [pltpu.make_async_copy(a, b, sems.at[i]) for i, (a, b) in enumerate(pairs)]
    for copy in copies:
        copy.start()
    for copy in copies:
        copy.wait()


def mine_kernel(w_ref, out_ref, sems):
    part = out_ref.shape[1] // 2
    me = lax.axis_index("dp")
    starts = (me & 1) * part, (2 + (me >> 1)) * part
    pairs = [
        (w_ref.at[:, pl.ds(pl.multiple_of(start, HEAD), part)], out_ref.at[:, pl.ds(i * part, part)])
        for i, start in enumerate(starts)
    ]
    copy_all(pairs, sems)


def pack_kernel(z1_ref, z2_ref, z3_ref, x_ref, y_ref):
    part = x_ref.shape[1]
    for m, piece in enumerate((z1_ref, z2_ref, z3_ref)):
        x_ref[pl.ds(m * HEAD, HEAD)] = piece[:, :part]
        y_ref[pl.ds(m * HEAD, HEAD)] = piece[:, part:]


def term_kernel(halves, r, at_ref, cot_ref, own_ref, *refs):
    count = len(halves)
    nears, near_cots, keeps, send_ref = refs[:count], refs[count : 2 * count], refs[2 * count : -1], refs[-1]
    rows, part = near_cots[0].shape
    half = part // 2
    x, y, z, c = at_ref[0] & 1, at_ref[0] >> 1, at_ref[2], at_ref[3]
    cots = []
    for b, near_cot in zip(halves, near_cots):
        place, inner = (x, y ^ r) if b == 0 else (2 + y, x ^ r)
        cots.append(
            (columns(cot_ref, place * part + inner * half, half), columns(near_cot, inner * half, half))
        )

    def make(i):
        n, i = i // 8, i % 8
        head = ((z ^ (i // 2)) * 2 + (c ^ (1 - i % 2))) * HEAD
        total = dot(columns(own_ref, head, HEAD)[:rows], cots[n][0], 0, 0)
        return total + dot(columns(nears[n], head, HEAD)[:rows], cots[n][1], 0, 0)

    def use(i, total):
        n, i = i // 8, i % 8
        if i % 2 == 1:
            keeps[n][i // 2] = total
        else:
            send_ref[n, i // 2] = total.astype(BF16)

    ahead(8 * count, make, use)


def rows_own_kernel(cot_ref, other_ref, own_ref, out_ref):
    rows = cot_ref.shape[0]
    out_ref[:rows] = dot(cot_ref[...], own_ref[...], 1, 1).astype(BF16)
    out_ref[rows:] = dot(other_ref[...], own_ref[...], 1, 1).astype(BF16)


def rows_early_kernel(at_ref, cot_ref, other_ref, z1_ref, z2_ref, out_ref):
    me, rows = at_ref[0], cot_ref.shape[0]
    part = z1_ref.shape[1] // 2
    x, y = me & 1, me >> 1
    pieces, tokens = (z1_ref, z2_ref), (cot_ref, other_ref)

    def make(i):
        piece, token = pieces[i % 2], tokens[i // 2]
        total = dot(columns(token, x * part, part), piece[:, :part], 1, 1)
        return total + dot(columns(token, (2 + y) * part, part), piece[:, part:], 1, 1)

    def use(i, total):
        out_ref[pl.ds(i // 2 * rows, rows), pl.ds(i % 2 * HEAD, HEAD)] = total

    ahead(4, make, use)


def rows_late_kernel(
    at_ref, cot_ref, other_ref, own_ref, early_ref, z3_ref, x_ref, y_ref, keep_ref, low_ref, high_ref
):
    me, z, rows = at_ref[0], at_ref[2], cot_ref.shape[0]
    part = x_ref.shape[1]
    x, y = me & 1, me >> 1
    order = (1, other_ref), (0, cot_ref)

    def make(i):
        token = order[i][1]
        total = dot(columns(token, (1 - x) * part, part), x_ref[...], 1, 1)
        total = total + dot(columns(token, (3 - y) * part, part), y_ref[...], 1, 1)
        third = dot(columns(token, x * part, part), z3_ref[:, :part], 1, 1)
        return total, third + dot(columns(token, (2 + y) * part, part), z3_ref[:, part:], 1, 1)

    def use(i, made):
        t, (total, third) = order[i][0], made
        here = pl.ds(t * rows, rows)
        heads = [
            own_ref[here, :],
            (total[:, :HEAD] + early_ref[here, :HEAD]).astype(BF16),
            (total[:, HEAD : 2 * HEAD] + early_ref[here, HEAD:]).astype(BF16),
            (total[:, 2 * HEAD :] + third).astype(BF16),
        ]
        for m, head in enumerate(heads):
            if t == 0:
                keep_ref[:, pl.ds(pl.multiple_of((z ^ m) * HEAD, HEAD), HEAD)] = head
            else:
                (low_ref, high_ref)[m // 2][:, m % 2 * HEAD : (m % 2 + 1) * HEAD] = head

    ahead(2, make, use)


def first_kernel(keep_ref, got_ref, odd_ref, even_ref):
    for m in range(4):
        (even_ref, odd_ref)[m % 2][m // 2] = (keep_ref[m] + got_ref[0, m].astype(F32)).astype(BF16)


def plane_kernel(b, odd, keep_ref, got_ref, level_ref, out_ref):
    for i in range(2):
        m = 2 * i + odd
        total = keep_ref[m] + got_ref[b, m].astype(F32) + level_ref[i].astype(F32)
        out_ref[i] = total.astype(out_ref.dtype)


def step_kernel(stay_ref, got_ref, total_ref, last_ref):
    total_ref[...] = stay_ref[0] + got_ref[0].astype(F32)
    last_ref[...] = (stay_ref[1] + got_ref[1].astype(F32)).astype(BF16)


def shard_kernel(scale, a_ref, got_a_ref, b_ref, got_b_ref, out_ref):
    half = a_ref.shape[1]
    out_ref[:, :half] = ((a_ref[...] + got_a_ref[...].astype(F32)) * scale).astype(BF16)
    out_ref[:, half:] = ((b_ref[...] + got_b_ref[...].astype(F32)) * scale).astype(BF16)


def place_kernel(at_ref, *refs):
    *pieces, out_ref, wide_ref, sems = refs
    half = pieces[0].shape[1] // 2
    copies = []
    for s, piece in enumerate(pieces):
        peer = at_ref[0] ^ s
        x, y = peer & 1, peer >> 1
        for b, start in enumerate((2 * x + y, 4 + 2 * y + x)):
            place = pl.ds(pl.multiple_of(start * half, half), half)
            wide_ref[2 * s + b] = piece[:, b * half : (b + 1) * half].astype(F32)
            copies.append(pltpu.make_async_copy(wide_ref.at[2 * s + b], out_ref.at[:, place], sems.at[2 * s + b]))
            copies[-1].start()
    for copy in copies:
        copy.wait()


def swap(value, axis, mask):
    size = lax.axis_size(axis)
    return lax.ppermute(value, axis, [(i, i ^ mask) for i in range(size)])


def plane_body(queries, keys, values, cotangent, w_out, counts, dests):
    rows, width = queries.shape
    depth = cotangent.shape[1]
    part, half = depth // 4, depth // 8
    me, f = lax.axis_index("dp"), lax.axis_index("fsdp")
    at = jnp.stack([me, f, f >> 1, f & 1]).astype(jnp.int32)
    tokens = rows * lax.axis_size("dp") * lax.axis_size("fsdp")

    cot_other = swap(cotangent, "fsdp", 1)
    to_x, to_y = call(
        quarters_kernel,
        [shaped(rows, part)] * 2,
        [cotangent],
        name="quarters",
        mib=4,
        in_specs=[ANY],
        scratch_shapes=[pltpu.SemaphoreType.DMA((2,))],
    )
    cot_x, cot_y = swap(to_x, "dp", 1), swap(to_y, "dp", 2)
    probs = probs_of(counts, queries, keys, mib=12)
    out = call(
        outputs_kernel,
        shaped(rows + HEADER, width),
        [counts, dests, probs, values],
        name="outputs",
        mib=8,
        after=[cot_other],
    )
    out_x, out_y = swap(out, "dp", 1), swap(out, "dp", 2)

    mine = call(
        mine_kernel,
        shaped(HEAD, 2 * part),
        [w_out],
        name="mine",
        mib=4,
        weight=MINE_WEIGHT,
        after=[to_x],
        in_specs=[ANY],
        out_specs=VMEM,
        scratch_shapes=[pltpu.SemaphoreType.DMA((2,))],
    )
    z2, z1 = swap(mine, "fsdp", 4), swap(mine, "fsdp", 2)
    z3 = swap(z2, "fsdp", 2)
    own = call(
        rows_own_kernel,
        shaped(2 * rows, HEAD),
        [cotangent, cot_other, w_out],
        name="rows_own",
        mib=12,
        after=[out],
    )

    far_rows = call(
        far_kernel,
        shaped(LMAX, width),
        [at, counts, dests, out],
        name="far",
        mib=8,
        after=[cot_x, cot_y],
    )

    turn = turned(probs, mib=8, weight=TURN_WEIGHT, after=[own, far_rows, z2])

    def term(halves, r, after):
        *keeps, send = call(
            functools.partial(term_kernel, halves, r),
            [shaped(4, HEAD, half, dtype=F32)] * len(halves) + [shaped(len(halves), 4, HEAD, half)],
            [at, cotangent, out]
            + [(out_x, out_y)[b] for b in halves]
            + [(cot_x, cot_y)[b] for b in halves],
            name="term" + "".join(str(b) for b in halves) + str(r),
            mib=14,
            after=after,
        )
        return keeps, swap(send, "fsdp", 1)

    keep_x, first_x = term([0], 1, [turn])
    keep_y, first_y = term([1], 1, keep_x + [z1])
    going = [
        call(
            first_kernel, [shaped(2, HEAD, half)] * 2, [*keep, got], name="first", mib=8
        )
        for keep, got in ((keep_x, first_x), (keep_y, first_y))
    ]
    odds = swap(going[0][0], "dp", 2), swap(going[1][0], "dp", 1)
    evens = swap(going[0][1], "dp", 2), swap(going[1][1], "dp", 1)
    going = [going[0][0], going[1][0]]
    keeps, second = term([0, 1], 0, going)

    early = call(
        rows_early_kernel,
        shaped(2 * rows, 2 * HEAD, dtype=F32),
        [at, cotangent, cot_other, z1, z2],
        name="rows_early",
        mib=12,
        weight=EARLY_WEIGHT,
        after=going,
    )
    three, three_token = call(
        attended_kernel,
        [shaped(4, LMAX, width), shaped(8, HEAD, dtype=F32)],
        [at, out, out_x, out_y],
        name="attended",
        mib=8,
        weight=ATTENDED_WEIGHT,
        after=going,
    )
    def plane(b, odd, level, dtype, after):
        return call(
            functools.partial(plane_kernel, b, odd),
            shaped(2, HEAD, half, dtype=dtype),
            [keeps[b], second, level],
            name="plane%d%d" % (b, odd),
            mib=8,
            after=after,
        )

    steps = [plane(b, 1, odds[b], BF16, [early]) for b in range(2)]
    stays = [plane(b, 0, evens[b], F32, steps) for b in range(2)]
    got = [swap(step, "fsdp", 2) for step in steps]

    to_x, to_y = call(
        pack_kernel,
        [shaped(3 * HEAD, part)] * 2,
        [z1, z2, z3],
        name="pack",
        mib=8,
        after=stays,
    )
    from_x, from_y = swap(to_x, "dp", 1), swap(to_y, "dp", 2)
    far = swap(far_rows, "dp", 3)

    totals, lasts = [], []
    for stay, step in zip(stays, got):
        total, last = call(
            step_kernel,
            [shaped(HEAD, half, dtype=F32), shaped(HEAD, half)],
            [stay, step],
            name="step",
            mib=4,
            weight=0 if totals else STEP_WEIGHT,

        )
        totals += [total, swap(last, "fsdp", 4)]
        lasts.append(last)

    attended, attended_token = call(
        across_kernel,
        [shaped(4, LMAX, width), shaped(8, HEAD, dtype=F32)],
        [three, far],
        name="across",
        mib=4,
        after=lasts,
        in_specs=[ANY, ANY],
        out_specs=[ANY, VMEM],
        scratch_shapes=[pltpu.SemaphoreType.DMA((1,))],
        input_output_aliases={0: 0},
    )
    shard = call(
        functools.partial(shard_kernel, float(tokens) ** -0.5),
        shaped(HEAD, part),
        totals,
        name="shard",
        mib=4,
        after=[attended_token],
    )
    across = swap(shard, "dp", 3)
    pieces = [shard, swap(shard, "dp", 1), swap(shard, "dp", 2), across]
    grad_keep, *grad_send = call(
        rows_late_kernel,
        [shaped(rows, width // 2)] + [shaped(rows, width // 4)] * 2,
        [at, cotangent, cot_other, own, early, z3, from_x, from_y],
        name="rows_late",
        after=[shard],
        mib=12,
    )
    grad_other = [swap(part, "fsdp", 1) for part in grad_send]
    *grads, token = backward(at, probs, turn, queries, keys, values, grad_keep, *grad_other)
    weight_grad = call(
        place_kernel,
        shaped(HEAD, depth, dtype=F32),
        [at, *pieces],
        name="place",
        after=[token],
        mib=8,
        out_specs=ANY,
        scratch_shapes=[pltpu.VMEM((8, HEAD, half), F32), pltpu.SemaphoreType.DMA((8,))],
    )
    return (*grads, attended[None, None], weight_grad)


def body(queries, keys, values, cotangent, w_out, counts, dests):
    rows, width = queries.shape
    groups = counts.shape[1]
    tokens = rows * lax.axis_size("dp") * lax.axis_size("fsdp")
    probs = probs_of(counts, queries, keys, mib=48)
    out, slots = call(
        slots_kernel,
        [shaped(rows, width), shaped(groups, LMAX, width)],
        [counts, dests, probs, values],
        name="slots",
        mib=48,
    )
    attended = lax.all_to_all(slots, "dp", split_axis=0, concat_axis=0, tiled=True)
    product = dot(out, cotangent, 0, 0) * float(tokens) ** -0.5
    shard = lax.psum_scatter(product.astype(BF16), "fsdp", scatter_dimension=0, tiled=True)
    weight_grad = lax.psum(shard, "dp").astype(F32)
    grad_rows = dot(cotangent, lax.all_gather(w_out, "fsdp", axis=0, tiled=True), 1, 1).astype(BF16)
    *grads, token = backward(None, probs, turned(probs, mib=48), queries, keys, values, grad_rows, mib=48)
    return (*grads, attended[None, None], weight_grad)


def solution(mesh):
    placed = (
        P(("dp", "fsdp"), None),
        P(("dp", "fsdp"), None),
        P(("dp", "fsdp"), None),
        P(("dp", "fsdp"), None),
        P("fsdp", None),
        P(("dp", "fsdp"), None),
        P(("dp", "fsdp"), None),
    )
    plane = mesh.shape["dp"] == 4 and mesh.shape["fsdp"] == HEADS
    return jax.shard_map(
        plane_body if plane else body,
        mesh=mesh,
        in_specs=placed,
        out_specs=(
            P(("dp", "fsdp"), None),
            P(("dp", "fsdp"), None),
            P(("dp", "fsdp"), None),
            P("dp", "fsdp", None, None, None),
            P("fsdp", None),
        ),
        check_vma=False,
    )
```
